256 devices in a mesh: lat: 8 (over x, core), lon: 32 (over z, y).
Axes of the slice: x: 4, y: 4, z: 8, core: 2. Of those that a mesh axis runs over, the one named last changes fastest.
Arguments:
- ensemble: float32 [96, 1536, 4, 128], P('lat', 'lon'), may hold values from -6 to 6
- grad_increment: float32 [96, 1536, 128], P('lat', 'lon'), may hold values from -6 to 6
- normalization: float32 [96, 1536], P('lat', 'lon'), may hold values from 12 to 48
- lon_diffusion: float32 [96, 1536], P('lat', 'lon'), may hold values from 1152 to 4608
- lat_diffusion: float32 [96, 1536], P('lat', 'lon'), may hold values from 288 to 1152
- vert_diag: float32 [128], replicated, may hold values from 1 to 2
- vert_sub: float32 [127], replicated, may hold values from -0.8 to -0.3
Outputs:
- grad_alpha: float32 [96, 1536, 4, 128], P('lat', 'lon')
The draws below stay inside these ranges and needn't reach their ends.
All inputs are finite; a program needn't handle non-finite values.
Results may differ from the reference program's by a relative error of at most 0.0003.
Values sent between devices are 32-bit elements; how exact they have to be, the bound alone decides.
A program may use at most 64 MiB of HBM per device.

```python
import math
import jax
import jax.numpy as jnp
from jax import lax

LEV = 128
MEMB = 4
NLAT = 96
NLON = 1536


def steps_of(stream_key, shape, shards, low, largest):
    def one(position, shards_of):
        heights = jax.random.uniform(jax.random.fold_in(jax.random.fold_in(stream_key, 6), position), (shards_of,), jnp.float32, low / len(shards), largest / len(shards))
        return jnp.repeat(jnp.exp(heights), shape[position] // shards_of).reshape((-1,) + (1,) * (len(shape) - position - 1))

    factor_of = one(*shards[0])
    for cut in shards[1:]:
        factor_of = factor_of * one(*cut)
    return factor_of


def bell_draw(key, dims, deviation, reach, split=(), kind=jnp.bfloat16):
    values = deviation * jax.random.normal(key, dims, jnp.float32)
    if split:
        values = values * steps_of(key, dims, split, -0.22, 0.18)
    return jnp.clip(values, -reach, reach).astype(kind)


def setup_inputs(seed: int = 0) -> dict:
    seeds = jax.random.split(jax.random.key(seed), 8)
    ensemble = bell_draw(seeds[0], (NLAT, NLON, MEMB, LEV), 1.0, 6.0, ((0, 8), (1, 32)), jnp.float32)
    grad_increment = bell_draw(seeds[1], (NLAT, NLON, LEV), 1.0, 6.0, ((0, 8), (1, 32)), jnp.float32)
    normalization = jnp.clip(jnp.exp(math.log(48.0) - 1.3862944 * jax.random.uniform(seeds[2], (NLAT, NLON), jnp.float32) ** steps_of(seeds[2], (NLAT, NLON), ((0, 8), (1, 32)), -0.2, 0.2)), 12.0, 48.0)
    lon_diffusion = jnp.clip(jnp.exp(math.log(4608.0) - 1.3862944 * jax.random.uniform(seeds[3], (NLAT, NLON), jnp.float32) ** steps_of(seeds[3], (NLAT, NLON), ((0, 8), (1, 32)), -0.2, 0.2)), 1152.0, 4608.0)
    lat_diffusion = jnp.clip(jnp.exp(math.log(1152.0) - 1.3862944 * jax.random.uniform(seeds[4], (NLAT, NLON), jnp.float32) ** steps_of(seeds[4], (NLAT, NLON), ((0, 8), (1, 32)), -0.2, 0.2)), 288.0, 1152.0)
    vert_diag = jnp.clip(jax.random.uniform(seeds[5], (LEV,), jnp.float32, 1.0, 2.0), 1.0, 2.0)
    vert_sub = jnp.clip(jax.random.uniform(seeds[6], (LEV - 1,), jnp.float32, -0.8, -0.3), -0.8, -0.3)
    return dict(ensemble=ensemble, grad_increment=grad_increment, normalization=normalization, lon_diffusion=lon_diffusion, lat_diffusion=lat_diffusion, vert_diag=vert_diag, vert_sub=vert_sub)


HIGHEST = lax.Precision.HIGHEST

def thomas_solve(diagonal, upper_band, rhs_vals):
    lower_band = jnp.concatenate([jnp.zeros_like(upper_band[:1]), upper_band[:-1]], axis=0)

    def forward(carry, item):
        ratio_prev, value_prev = carry
        diag_now, low_now, up_now, rhs_now = item
        pivot_val = diag_now - low_now * ratio_prev
        ratio_now = up_now / pivot_val
        value_now = (rhs_now - low_now[:, None] * value_prev) / pivot_val[:, None]
        return ((ratio_now, value_now), (ratio_now, value_now))
    start = (jnp.zeros_like(diagonal[0]), jnp.zeros_like(rhs_vals[0]))
    _, (ratio_all, value_all) = lax.scan(forward, start, (diagonal, lower_band, upper_band, rhs_vals))

    def backward(next_val, item):
        ratio_now, value_now = item
        result = value_now - ratio_now[:, None] * next_val
        return (result, result)
    _, solved = lax.scan(backward, jnp.zeros_like(rhs_vals[0]), (ratio_all, value_all), reverse=True)
    return solved

def longitude_solve(weighted, lon_diffusion):
    coeff_t = jnp.transpose(lon_diffusion)
    diagonal = 1.0 + jnp.roll(coeff_t, 1, axis=0) + coeff_t
    corner = -coeff_t[-1]
    gamma_val = -diagonal[0]
    diag_mod = jnp.concatenate([(diagonal[0] - gamma_val)[None], diagonal[1:-1], (diagonal[-1] - corner * corner / gamma_val)[None]], axis=0)
    upper_band = jnp.concatenate([-coeff_t[:-1], jnp.zeros_like(coeff_t[:1])], axis=0)
    rhs_t = jnp.transpose(weighted, (1, 0, 2))
    first_sol = thomas_solve(diag_mod, upper_band, rhs_t)
    middle = jnp.zeros((coeff_t.shape[0] - 2, coeff_t.shape[1], 1), coeff_t.dtype)
    update_vec = jnp.concatenate([gamma_val[None, :, None], middle, corner[None, :, None]], axis=0)
    second_sol = thomas_solve(diag_mod, upper_band, update_vec)
    factor_ratio = (corner / gamma_val)[:, None]
    dot_first = first_sol[0] + factor_ratio * first_sol[-1]
    dot_second = second_sol[0] + factor_ratio * second_sol[-1]
    solved = first_sol - second_sol * (dot_first / (1.0 + dot_second))[None]
    return jnp.transpose(solved, (1, 0, 2))

def latitude_solve(along_lon, lat_diffusion):
    lat_total = lat_diffusion.shape[0]
    row_ids = jnp.arange(lat_total).astype(lat_diffusion.dtype)
    latitude = -jnp.pi / 2 + (row_ids + 0.5) * jnp.pi / lat_total
    cosine = jnp.cos(latitude)
    edge_keep = (jnp.arange(lat_total) < lat_total - 1).astype(lat_diffusion.dtype)
    coeff = lat_diffusion * edge_keep[:, None]
    before = jnp.concatenate([jnp.zeros_like(coeff[:1]), coeff[:-1]], axis=0)
    diagonal = cosine[:, None] + before + coeff
    solved = thomas_solve(diagonal, -coeff, along_lon)
    return cosine[:, None, None] * solved

def vertical_inverse(vert_diag, vert_sub):
    factor = jnp.diag(vert_diag) + jnp.diag(vert_sub, -1)
    identity = jnp.eye(vert_diag.shape[0], dtype=vert_diag.dtype)
    return jax.scipy.linalg.cho_solve((factor, True), identity)

def reference(ensemble, grad_increment, normalization, lon_diffusion, lat_diffusion, vert_diag, vert_sub):
    lat_total, lon_total, members, levels = ensemble.shape
    weighted = normalization[:, :, None, None] * ensemble * grad_increment[:, :, None, :]
    weighted = weighted.reshape(lat_total, lon_total, members * levels)
    along_lon = longitude_solve(weighted, lon_diffusion)
    along_lat = latitude_solve(along_lon, lat_diffusion)
    along_lat = along_lat.reshape(lat_total, lon_total, members, levels)
    inverse = vertical_inverse(vert_diag, vert_sub)
    return jnp.einsum('abml,lk->abmk', along_lat, inverse, precision=HIGHEST)
```

```python
import functools
import math

import jax
import jax.numpy as jnp
from jax import lax
from jax.experimental import pallas as pl
from jax.experimental.pallas import tpu as pltpu
from jax.sharding import PartitionSpec as P

HIGHEST = lax.Precision.HIGHEST
MESH = pl.DeviceIdType.MESH
F32 = jnp.float32

ROWS, COLS, MEMB, LEV = 12, 48, 4, 128
BANDS, BLOCKS = 8, 32
SUB = 8
RUN = COLS // SUB
UNITS = MEMB * RUN
SHARE = UNITS // BANDS
NLAT = ROWS * BANDS
HALF = SHARE * SUB


def solver_of(row, core):
    return ((2 * row + core) * 4) // 3


def rows_at(start, count=SUB):
    return pl.ds(pl.multiple_of(start, SUB), count)


def wide(row, rows=SUB):
    return jnp.broadcast_to(row, (rows, LEV))


def sublane_sums(vals):
    sub = lax.broadcasted_iota(jnp.int32, (SUB, LEV), 0)
    low = sub < 4
    four = [
        jnp.where(low, vals[k], vals[k + 4]) + pltpu.roll(jnp.where(low, vals[k + 4], vals[k]), 4, 0)
        for k in range(4)
    ]
    low = sub % 4 < 2
    two = [
        jnp.where(low, four[k] + pltpu.roll(four[k], 6, 0), four[k + 2] + pltpu.roll(four[k + 2], 2, 0))
        for k in range(2)
    ]
    low = sub % 2 < 1
    return jnp.where(low, two[0] + pltpu.roll(two[0], 7, 0), two[1] + pltpu.roll(two[1], 1, 0))


def sums_before(val):
    sub = lax.broadcasted_iota(jnp.int32, (SUB, LEV), 0)
    val = jnp.where(sub >= 1, pltpu.roll(val, 1, 0), 0.0)
    for step in (1, 2, 4):
        val = val + jnp.where(sub >= step, pltpu.roll(val, step, 0), 0.0)
    return val


def sums_after(val):
    sub = lax.broadcasted_iota(jnp.int32, (SUB, LEV), 0)
    val = jnp.where(sub < SUB - 1, pltpu.roll(val, SUB - 1, 0), 0.0)
    for step in (1, 2, 4):
        val = val + jnp.where(sub < SUB - step, pltpu.roll(val, SUB - step, 0), 0.0)
    return val


def kernel(
    e_hbm, g_hbm, norm_ref, lon_ref, lat_ref, diag_ref, below_ref, out_hbm,
    e_v, g_v, out_v, y_v,
    tmp, rk_t, phi_t, w1_t, n_t, phin_t, w1n_t,
    w1n_e, phin_e, w1_e, phi_e,
    lat_pad, lat_rk, lat_rows, lat_t, w1l_e, phil_e, cw1_e, cphi_e,
    vinv,
    cs_a, cr_a, ss_a, sr_a, ts_a, tr_a, rows_a, inv_a,
    cs_b, cr_b, ss_b, sr_b, ts_b, tr_b, rows_b, tb_b, el_b,
    load_sem, store_sem,
    ca_send, ca_recv, sa_send, sa_recv, ta_send, ta_recv,
    cb_send, cb_recv, sb_send, sb_recv, tb_send, tb_recv,
):
    band = lax.axis_index("lat")
    me = lax.axis_index("lon")
    core = band % 2
    place = me - me // 4
    is_solver = jnp.logical_and(me % 4 != 3, place % 2 == core)
    my_row = place // 2

    loads = [
        pltpu.make_async_copy(g_hbm, g_v, load_sem.at[0]),
        pltpu.make_async_copy(e_hbm, e_v, load_sem.at[1]),
    ]
    for copy in loads:
        copy.start()

    barrier = pltpu.get_barrier_semaphore()

    def greet_lon(step, _):
        pl.semaphore_signal(barrier, inc=1, device_id=(band, (me + step) % BLOCKS), device_id_type=MESH)
        return 0

    def greet_lat(step, _):
        pl.semaphore_signal(barrier, inc=1, device_id=((band + step) % BANDS, me), device_id_type=MESH)
        return 0

    lax.fori_loop(1, BLOCKS, greet_lon, 0)
    lax.fori_loop(1, BANDS, greet_lat, 0)

    tmp[...] = jnp.full((LEV, LEV), 2048.0, F32)
    tmp[0:ROWS, 0:COLS] = lon_ref[...]
    rk_t[...] = 1.0 / tmp[...].T[0:COLS]
    tmp[0:ROWS, 0:COLS] = norm_ref[...]
    n_t[...] = tmp[...].T[0:COLS]
    flow_p = jnp.zeros((1, LEV), F32)
    flow_s = jnp.zeros((1, LEV), F32)
    val_p = rk_t[0:1]
    val_s = rk_t[COLS - 1 : COLS]
    phi_t[0:1] = jnp.zeros((1, LEV), F32)
    phi_t[1:2] = val_p
    w1_t[COLS - 1 : COLS] = val_s
    for i in range(1, COLS):
        flow_p = flow_p + val_p
        val_p = val_p + (1.0 + flow_p) * rk_t[i : i + 1]
        if i < COLS - 1:
            phi_t[i + 1 : i + 2] = val_p
        k = COLS - i
        flow_s = flow_s + val_s
        val_s = val_s + (1.0 + flow_s) * rk_t[k - 1 : k]
        w1_t[k - 1 : k] = val_s
    edge = 1.0 / val_p
    scale = 1.0 / val_s
    cs_a[...] = jnp.zeros((SUB, LEV), F32)
    cs_a[0:1] = edge
    cs_a[1:2] = 1.0 + flow_s * scale
    cs_a[2:3] = flow_p * edge
    w1_t[...] = w1_t[...] * scale
    w1n_t[...] = w1_t[...] * n_t[...]
    phin_t[...] = phi_t[...] * n_t[...]

    pl.semaphore_wait(barrier, BLOCKS + BANDS - 2)

    def coeff_copy_a(row):
        return pltpu.make_async_remote_copy(
            src_ref=cs_a,
            dst_ref=cr_a.at[rows_at(me * SUB)],
            send_sem=ca_send.at[row],
            recv_sem=ca_recv,
            device_id=(band, solver_of(row, core)),
            device_id_type=MESH,
        )

    def rhs_copy_a(row):
        return pltpu.make_async_remote_copy(
            src_ref=ss_a.at[rows_at(row * SUB)],
            dst_ref=sr_a.at[rows_at(me * SUB)],
            send_sem=sa_send.at[row],
            recv_sem=sa_recv,
            device_id=(band, solver_of(row, core)),
            device_id_type=MESH,
        )

    def back_copy_a(target):
        return pltpu.make_async_remote_copy(
            src_ref=ts_a.at[rows_at(target * SUB)],
            dst_ref=tr_a.at[rows_at(my_row * SUB)],
            send_sem=ta_send.at[target],
            recv_sem=ta_recv.at[my_row],
            device_id=(band, target),
            device_id_type=MESH,
        )

    def copy_b(kind, target):
        size = SUB if kind == 0 else 2 * HALF
        source = (cs_b, ss_b, ts_b)[kind]
        dest = (cr_b, sr_b, tr_b)[kind]
        return pltpu.make_async_remote_copy(
            src_ref=source if kind == 0 else source.at[rows_at(target * size, size)],
            dst_ref=dest.at[rows_at(band * size, size)],
            send_sem=(cb_send, sb_send, tb_send)[kind].at[target],
            recv_sem=(cb_recv, sb_recv, tb_recv)[kind].at[band],
            device_id=(target, me),
            device_id_type=MESH,
        )

    def landed_b(kind, source):
        size = SUB if kind == 0 else 2 * HALF
        dest = (cr_b, sr_b, tr_b)[kind]
        slot = dest.at[rows_at(source * size, size)]
        return pltpu.make_async_copy(slot, slot, (cb_recv, sb_recv, tb_recv)[kind].at[source])

    def send_coeff_a(step, _):
        row = (me + step) % ROWS

        @pl.when(solver_of(row, core) != me)
        def _():
            coeff_copy_a(row).start()

        return 0

    lax.fori_loop(0, ROWS, send_coeff_a, 0)

    @pl.when(is_solver)
    def _():
        cr_a[rows_at(me * SUB)] = cs_a[...]

    lat_pad[...] = jnp.full((16, LEV), 512.0, F32)
    lat_pad[0:ROWS, 0:COLS] = lat_ref[...]
    lat_rk[...] = 1.0 / lat_pad[...]
    at = band * ROWS + lax.broadcasted_iota(jnp.int32, (16, LEV), 0)
    at = jnp.minimum(at, NLAT - 1 - at).astype(F32)
    angle = (at + 0.5) * (math.pi / NLAT)
    square = angle * angle
    series = jnp.full((16, LEV), 1.0 / math.factorial(13), F32)
    for power in (11, 9, 7, 5, 3, 1):
        series = 1.0 / math.factorial(power) - series * square
    lat_t[0:16] = angle * series

    def cosine(j):
        return lat_t[j : j + 1]

    last = jnp.where(band == BANDS - 1, 0.0, 1.0) * lat_pad[ROWS - 1 : ROWS]
    lat_rows[...] = jnp.zeros((LEV, LEV), F32)
    flow_p = jnp.zeros((1, LEV), F32)
    flow_s = jnp.zeros((1, LEV), F32)
    val_p = lat_rk[0:1]
    val_s = jnp.ones((1, LEV), F32)
    lat_rows[17:18] = val_p
    lat_rows[ROWS - 1 : ROWS] = val_s
    for j in range(1, ROWS):
        flow_p = flow_p + cosine(j) * val_p
        if j < ROWS - 1:
            val_p = val_p + (1.0 + flow_p) * lat_rk[j : j + 1]
            lat_rows[17 + j : 18 + j] = val_p
        k = ROWS - j
        flow_s = flow_s + cosine(k) * val_s
        val_s = val_s + (last + flow_s) * lat_rk[k - 1 : k]
        lat_rows[k - 1 : k] = val_s
    edge = last / (last * val_p + 1.0 + flow_p)
    scale = 1.0 / val_s
    cs_b[...] = jnp.zeros((SUB, LEV), F32)
    cs_b[0:1] = edge
    cs_b[1:2] = cosine(0) + flow_s * scale
    cs_b[2:3] = flow_p * edge
    lat_rows[0:16] = lat_rows[0:16] * scale
    lat_rows[32:48] = lat_rows[0:16] * lat_t[0:16]
    lat_rows[48:64] = lat_rows[16:32] * lat_t[0:16]

    def send_coeff_b(step, _):
        copy_b(0, (band + step) % BANDS).start()
        return 0

    lax.fori_loop(1, BANDS, send_coeff_b, 0)
    cr_b[rows_at(band * SUB)] = cs_b[...]

    for t in range(RUN):
        for source, target in ((w1n_t, w1n_e), (phin_t, phin_e)):
            part = source[pl.ds(t, SUB, stride=RUN), :]
            for j in range(ROWS):
                at = j * COLS + t * SUB
                target[at : at + SUB] = jnp.broadcast_to(part[:, j : j + 1], (SUB, LEV))

    for copy in loads:
        copy.wait()

    def contribute(step, _):
        row = (me + step) % ROWS
        sums = [jnp.zeros((SUB, LEV), F32) for _ in range(2 * MEMB)]
        for t in range(RUN):
            grad = g_v[pl.ds(row * COLS + t, SUB, stride=RUN), :]
            first = w1n_e[rows_at(row * COLS + t * SUB)] * grad
            second = phin_e[rows_at(row * COLS + t * SUB)] * grad
            for m in range(MEMB):
                value = e_v[pl.ds(row * COLS * MEMB + t * MEMB + m, SUB, stride=RUN * MEMB), :]
                sums[m] = sums[m] + first * value
                sums[MEMB + m] = sums[MEMB + m] + second * value
        ss_a[rows_at(row * SUB)] = sublane_sums(sums)

        @pl.when(solver_of(row, core) != me)
        def _():
            rhs_copy_a(row).start()

        return 0

    lax.fori_loop(0, ROWS, contribute, 0)

    @pl.when(is_solver)
    def _():
        sr_a[rows_at(me * SUB)] = ss_a[rows_at(my_row * SUB)]

    tmp[0:SUB] = jnp.zeros((SUB, LEV), F32)
    tmp[0:1, 0 : LEV - 1] = below_ref[...]
    dinv = 1.0 / wide(diag_ref[...])
    lane = lax.broadcasted_iota(jnp.int32, (SUB, LEV), 1)
    ratio = jnp.where(lane == 0, 0.0, -pltpu.roll(wide(tmp[0:1]), 1, 1) * dinv)
    row_ids = lax.broadcasted_iota(jnp.int32, (LEV, LEV), 0)
    col_ids = lax.broadcasted_iota(jnp.int32, (LEV, LEV), 1)
    half = jnp.where(row_ids == col_ids, wide(dinv[0:1], LEV), 0.0)
    step = 1
    while step < LEV:
        half = half + wide(ratio[0:1], LEV) * pltpu.roll(half, step, 1)
        ratio = ratio * pltpu.roll(ratio, step, 1)
        step *= 2
    vinv[...] = lax.dot_general(
        half, half, (((1,), (1,)), ((), ())), precision=HIGHEST, preferred_element_type=F32
    )

    @pl.when(is_solver)
    def _():
        slots = cr_a.at[rows_at(0, (BLOCKS - 1) * SUB)]
        pltpu.make_async_copy(slots, slots, ca_recv).wait()
        link = cr_a[pl.ds(0, BLOCKS, stride=SUB), :]
        base = cr_a[pl.ds(1, BLOCKS, stride=SUB), :] + pltpu.roll(cr_a[pl.ds(2, BLOCKS, stride=SUB), :], 1, 0)
        rows_a[0:BLOCKS] = 1.0 / link
        rows_a[BLOCKS : 2 * BLOCKS] = base
        flow_p = jnp.zeros((1, LEV), F32)
        flow_s = jnp.zeros((1, LEV), F32)
        val_p = rows_a[0:1]
        val_s = rows_a[BLOCKS - 1 : BLOCKS]
        tmp[0:1] = jnp.zeros((1, LEV), F32)
        tmp[1:2] = val_p
        tmp[2 * BLOCKS - 1 : 2 * BLOCKS] = val_s
        for p in range(1, BLOCKS):
            flow_p = flow_p + rows_a[BLOCKS + p : BLOCKS + p + 1] * val_p
            val_p = val_p + (1.0 + flow_p) * rows_a[p : p + 1]
            if p < BLOCKS - 1:
                tmp[p + 1 : p + 2] = val_p
            k = BLOCKS - p
            flow_s = flow_s + rows_a[BLOCKS + k : BLOCKS + k + 1] * val_s
            val_s = val_s + (1.0 + flow_s) * rows_a[k - 1 : k]
            tmp[BLOCKS + k - 1 : BLOCKS + k] = val_s
        first = tmp[BLOCKS : 2 * BLOCKS] * (1.0 / val_s)
        both = first + tmp[0:BLOCKS] * (1.0 / val_p)
        total = jnp.sum(both * base, axis=0, keepdims=True)
        tmp[BLOCKS : 2 * BLOCKS] = first
        tmp[2 * BLOCKS : 3 * BLOCKS] = both * (1.0 / total)
        tmp[3 * BLOCKS : 4 * BLOCKS] = both
        whole = tmp[...]
        lanes = lax.broadcasted_iota(jnp.int32, (LEV, LEV), 1)
        column = jnp.sum(jnp.where(lanes == my_row, whole, 0.0), axis=1, keepdims=True)
        column = jnp.broadcast_to(column, (LEV, LEV))
        tmp[...] = whole.T
        line = wide(tmp[pl.ds(my_row, 1), :])
        phi_row = wide(line[0:1], BLOCKS)
        first_row = wide(pltpu.roll(line, LEV - BLOCKS, 1)[0:1], BLOCKS)
        both_row = wide(pltpu.roll(line, LEV - 2 * BLOCKS, 1)[0:1], BLOCKS)
        sub_ids = lax.broadcasted_iota(jnp.int32, (BLOCKS, LEV), 0)
        lane_ids = lax.broadcasted_iota(jnp.int32, (BLOCKS, LEV), 1)
        inv_a[0:BLOCKS] = (
            jnp.where(
                sub_ids <= lane_ids,
                column[0:BLOCKS] * first_row,
                column[BLOCKS : 2 * BLOCKS] * phi_row,
            )
            + column[3 * BLOCKS : 4 * BLOCKS] * both_row
        )
        link = jnp.sum(jnp.where(lane_ids == my_row, link, 0.0), axis=1, keepdims=True)
        inv_a[BLOCKS : 2 * BLOCKS] = jnp.broadcast_to(link, (BLOCKS, LEV))

    @pl.when(is_solver)
    def _():
        slots = sr_a.at[rows_at(0, (BLOCKS - 1) * SUB)]
        pltpu.make_async_copy(slots, slots, sa_recv).wait()
        link = inv_a[BLOCKS : 2 * BLOCKS]
        inverse = inv_a[0:BLOCKS][:, 0:BLOCKS]
        for m in range(MEMB):
            own = sr_a[pl.ds(m, BLOCKS, stride=SUB), :]
            after = sr_a[pl.ds(MEMB + m, BLOCKS, stride=SUB), :]
            rhs = own + pltpu.roll(link * after, 1, 0)
            rhs = jnp.dot(rhs, vinv[...], precision=HIGHEST, preferred_element_type=F32)
            found = jnp.dot(inverse, rhs, precision=HIGHEST, preferred_element_type=F32)
            ts_a[pl.ds(m, BLOCKS, stride=SUB), :] = found
            ts_a[pl.ds(MEMB + m, BLOCKS, stride=SUB), :] = link * pltpu.roll(found, BLOCKS - 1, 0)

        def send_back(step, _):
            back_copy_a((me + step) % BLOCKS).start()
            return 0

        lax.fori_loop(1, BLOCKS, send_back, 0)
        tr_a[rows_at(my_row * SUB)] = ts_a[rows_at(me * SUB)]

    for t in range(RUN):
        for source, target in ((w1_t, w1_e), (phi_t, phi_e)):
            part = source[pl.ds(t, SUB, stride=RUN), :]
            for j in range(ROWS):
                at = j * COLS + t * SUB
                target[at : at + SUB] = jnp.broadcast_to(part[:, j : j + 1], (SUB, LEV))

    def interior(row, _):
        firsts, seconds = [], []
        for t in range(RUN):
            grad = g_v[pl.ds(row * COLS + t, SUB, stride=RUN), :]
            firsts.append(w1n_e[rows_at(row * COLS + t * SUB)] * grad)
            seconds.append(phin_e[rows_at(row * COLS + t * SUB)] * grad)
        for m in range(MEMB):
            values = [
                e_v[pl.ds(row * COLS * MEMB + t * MEMB + m, SUB, stride=RUN * MEMB), :] for t in range(RUN)
            ]
            ahead = [seconds[0] * values[0]]
            for t in range(1, RUN):
                ahead.append(ahead[-1] + seconds[t] * values[t])
            behind = [None] * RUN
            total = jnp.zeros((SUB, LEV), F32)
            for t in reversed(range(RUN)):
                behind[t] = total
                total = total + firsts[t] * values[t]
            before = sums_before(ahead[-1])
            after = sums_after(total)
            for t in range(RUN):
                w1 = w1_e[rows_at(row * COLS + t * SUB)]
                phi = phi_e[rows_at(row * COLS + t * SUB)]
                y_v[rows_at(((m * RUN + t) * ROWS + row) * SUB)] = w1 * (before + ahead[t]) + phi * (
                    after + behind[t]
                )
        return 0

    lax.fori_loop(0, ROWS, interior, 0)

    size = UNITS * SUB

    def vertical(part, _):
        at = rows_at(part * size, size)
        y_v[at] = jnp.dot(y_v[at], vinv[...], precision=HIGHEST, preferred_element_type=F32)
        return 0

    lax.fori_loop(0, ROWS, vertical, 0)

    lat_t[...] = lat_rows[...].T
    for t in range(RUN):
        part = lat_t[pl.ds(t, SUB, stride=RUN), :]
        for number, target in enumerate((w1l_e, phil_e, cw1_e, cphi_e)):
            for j in range(ROWS):
                at = j * COLS + t * SUB
                lane_at = number * 16 + j
                target[at : at + SUB] = jnp.broadcast_to(part[:, lane_at : lane_at + 1], (SUB, LEV))

    def wait_coeff_b(step, _):
        landed_b(0, (band + step) % BANDS).wait()
        return 0

    lax.fori_loop(1, BANDS, wait_coeff_b, 0)
    flow_p = jnp.zeros((1, LEV), F32)
    flow_s = jnp.zeros((1, LEV), F32)
    val_p = jnp.ones((1, LEV), F32)
    val_s = jnp.ones((1, LEV), F32)

    def band_base(p):
        own = cr_b[p * SUB + 1 : p * SUB + 2]
        return own if p == 0 else own + cr_b[(p - 1) * SUB + 2 : (p - 1) * SUB + 3]

    def band_link(p):
        return cr_b[p * SUB : p * SUB + 1]

    rows_b[...] = jnp.zeros((LEV, LEV), F32)
    rows_b[0:1] = val_p
    rows_b[2 * BANDS - 1 : 2 * BANDS] = val_s
    for p in range(BANDS - 1):
        flow_p = flow_p + band_base(p) * val_p
        val_p = val_p + flow_p / band_link(p)
        rows_b[p + 1 : p + 2] = val_p
        k = BANDS - 1 - p
        flow_s = flow_s + band_base(k) * val_s
        val_s = val_s + flow_s / band_link(k - 1)
        rows_b[BANDS + k - 1 : BANDS + k] = val_s
    flow_s = flow_s + band_base(0) * val_s
    rows_b[BANDS : 2 * BANDS] = rows_b[BANDS : 2 * BANDS] * (1.0 / flow_s)
    for p in range(BANDS - 1):
        rows_b[2 * BANDS + p : 2 * BANDS + p + 1] = band_link(p)
    tb_b[...] = rows_b[...].T
    for tt in range(SHARE):
        part = tb_b[pl.ds((band % 2) * SHARE + tt, SUB, stride=RUN), :]
        for number in range(3 * BANDS):
            at = (number * SHARE + tt) * SUB
            el_b[at : at + SUB] = jnp.broadcast_to(part[:, number : number + 1], (SUB, LEV))

    def wait_back_a(row, _):
        @pl.when(solver_of(row, core) != me)
        def _():
            slot = tr_a.at[rows_at(row * SUB)]
            pltpu.make_async_copy(slot, slot, ta_recv.at[row]).wait()

        return 0

    lax.fori_loop(0, ROWS, wait_back_a, 0)

    def finish_lon(step, _):
        share = (band + 1 + step) % BANDS
        m = share // 2
        for tt in range(SHARE):
            t = (share % 2) * SHARE + tt
            own = jnp.zeros((SUB, LEV), F32)
            after = jnp.zeros((SUB, LEV), F32)
            for j in range(ROWS):
                at = rows_at(((share * SHARE + tt) * ROWS + j) * SUB)
                coeff = rows_at(j * COLS + t * SUB)
                sep_own = wide(tr_a[pl.ds(j * SUB + m, 1), :])
                sep_next = wide(tr_a[pl.ds(j * SUB + MEMB + m, 1), :])
                value = y_v[at] + w1_e[coeff] * sep_own + phi_e[coeff] * sep_next
                y_v[at] = value
                own = own + w1l_e[coeff] * value
                after = after + phil_e[coeff] * value
            ss_b[rows_at(share * 2 * HALF + tt * SUB)] = own
            ss_b[rows_at(share * 2 * HALF + HALF + tt * SUB)] = after

        @pl.when(share != band)
        def _():
            copy_b(1, share).start()

        return 0

    lax.fori_loop(0, BANDS, finish_lon, 0)
    sr_b[rows_at(band * 2 * HALF, 2 * HALF)] = ss_b[rows_at(band * 2 * HALF, 2 * HALF)]

    def interior_lat(unit, _):
        t = unit % RUN
        total = jnp.zeros((SUB, LEV), F32)
        aheads = []
        for j in range(ROWS):
            at = rows_at((unit * ROWS + j) * SUB)
            total = total + phil_e[rows_at(j * COLS + t * SUB)] * y_v[at]
            aheads.append(total)
        total = jnp.zeros((SUB, LEV), F32)
        for j in reversed(range(ROWS)):
            at = rows_at((unit * ROWS + j) * SUB)
            coeff = rows_at(j * COLS + t * SUB)
            value = y_v[at]
            y_v[at] = cw1_e[coeff] * aheads[j] + cphi_e[coeff] * total
            total = total + w1l_e[coeff] * value
        return 0

    lax.fori_loop(0, UNITS, interior_lat, 0)

    def wait_rhs_b(step, _):
        landed_b(1, (band + step) % BANDS).wait()
        return 0

    lax.fori_loop(1, BANDS, wait_rhs_b, 0)

    for tt in range(SHARE):

        def spread(number):
            at = (number * SHARE + tt) * SUB
            return el_b[at : at + SUB]

        rhs = []
        total = jnp.zeros((SUB, LEV), F32)
        aheads = []
        for p in range(BANDS):
            at = p * 2 * HALF + tt * SUB
            value = sr_b[at : at + SUB]
            if p > 0:
                before = at - HALF
                value = value + spread(2 * BANDS + p - 1) * sr_b[before : before + SUB]
            rhs.append(value)
            total = total + spread(p) * value
            aheads.append(total)
        total = jnp.zeros((SUB, LEV), F32)
        found = None
        for p in reversed(range(BANDS)):
            at = p * 2 * HALF + tt * SUB
            if p == BANDS - 1:
                ts_b[at + HALF : at + HALF + SUB] = jnp.zeros((SUB, LEV), F32)
            else:
                ts_b[at + HALF : at + HALF + SUB] = spread(2 * BANDS + p) * found
            found = spread(BANDS + p) * aheads[p] + spread(p) * total
            ts_b[at : at + SUB] = found
            total = total + spread(BANDS + p) * rhs[p]

    def send_back_b(step, _):
        copy_b(2, (band + step) % BANDS).start()
        return 0

    lax.fori_loop(1, BANDS, send_back_b, 0)
    tr_b[rows_at(band * 2 * HALF, 2 * HALF)] = ts_b[rows_at(band * 2 * HALF, 2 * HALF)]

    def finish(step, _):
        share = (band + step) % BANDS

        @pl.when(share != band)
        def _():
            landed_b(2, share).wait()

        m = share // 2
        for tt in range(SHARE):
            t = (share % 2) * SHARE + tt
            sep_own = tr_b[rows_at(share * 2 * HALF + tt * SUB)]
            sep_next = tr_b[rows_at(share * 2 * HALF + HALF + tt * SUB)]
            for j in range(ROWS):
                at = rows_at(((share * SHARE + tt) * ROWS + j) * SUB)
                coeff = rows_at(j * COLS + t * SUB)
                out_v[pl.ds(j * COLS * MEMB + t * MEMB + m, SUB, stride=RUN * MEMB), :] = (
                    y_v[at] + cw1_e[coeff] * sep_own + cphi_e[coeff] * sep_next
                )
        return 0

    lax.fori_loop(0, BANDS, finish, 0)
    result = pltpu.make_async_copy(out_v, out_hbm, store_sem)
    result.start()

    def sent_a(row, _):
        @pl.when(solver_of(row, core) != me)
        def _():
            coeff_copy_a(row).wait_send()
            rhs_copy_a(row).wait_send()

        return 0

    lax.fori_loop(0, ROWS, sent_a, 0)

    @pl.when(is_solver)
    def _():
        def sent_back(step, _):
            back_copy_a((me + step) % BLOCKS).wait_send()
            return 0

        lax.fori_loop(1, BLOCKS, sent_back, 0)

    def sent_b(step, _):
        for kind in range(3):
            copy_b(kind, (band + step) % BANDS).wait_send()
        return 0

    lax.fori_loop(1, BANDS, sent_b, 0)
    result.wait()


def shards(
    ensemble, grad_increment, normalization, lon_diffusion, lat_diffusion, vert_diag, vert_sub
):
    block = ROWS * COLS * MEMB
    vmem = pl.BlockSpec(memory_space=pltpu.VMEM)
    anywhere = pl.BlockSpec(memory_space=pl.ANY)

    def buf(rows):
        return pltpu.VMEM((rows, LEV), F32)

    coeffs = ROWS * COLS
    dma = pltpu.SemaphoreType.DMA
    scratch = [
        buf(block), buf(coeffs), buf(block), buf(block),
        buf(LEV), *[buf(COLS)] * 6,
        *[buf(coeffs)] * 4,
        buf(16), buf(16), buf(LEV), buf(LEV), *[buf(coeffs)] * 4,
        buf(LEV),
        buf(SUB), buf(BLOCKS * SUB), buf(ROWS * SUB), buf(BLOCKS * SUB), buf(BLOCKS * SUB), buf(ROWS * SUB),
        buf(2 * BLOCKS), buf(2 * BLOCKS),
        buf(SUB), buf(BANDS * SUB), *[buf(BANDS * 2 * HALF)] * 4,
        buf(LEV), buf(LEV), buf(3 * BANDS * HALF),
        dma((2,)), dma,
        dma((ROWS,)), dma, dma((ROWS,)), dma, dma((BLOCKS,)), dma((ROWS,)),
        *[dma((BANDS,))] * 6,
    ]
    out = pl.pallas_call(
        kernel,
        out_shape=jax.ShapeDtypeStruct((block, LEV), F32),
        in_specs=[anywhere, anywhere, vmem, vmem, vmem, vmem, vmem],
        out_specs=anywhere,
        scratch_shapes=scratch,
        compiler_params=pltpu.CompilerParams(
            collective_id=0, has_side_effects=True, vmem_limit_bytes=32 * 1024 * 1024
        ),
    )(
        ensemble.reshape(block, LEV),
        grad_increment.reshape(coeffs, LEV),
        normalization,
        lon_diffusion,
        lat_diffusion,
        vert_diag.reshape(1, LEV),
        vert_sub.reshape(1, LEV - 1),
    )
    return out.reshape(ROWS, COLS, MEMB, LEV)


def solution(mesh):
    in_specs = (
        P("lat", "lon", None, None),
        P("lat", "lon", None),
        P("lat", "lon"),
        P("lat", "lon"),
        P("lat", "lon"),
        P(),
        P(),
    )
    out_specs = P("lat", "lon", None, None)
    return jax.shard_map(shards, mesh=mesh, in_specs=in_specs, out_specs=out_specs, check_vma=False)
```

```python
import functools
import math

import jax
import jax.numpy as jnp
from jax import lax
from jax.experimental import pallas as pl
from jax.experimental.pallas import tpu as pltpu
from jax.sharding import PartitionSpec as P

HIGHEST = lax.Precision.HIGHEST
MESH = pl.DeviceIdType.MESH
F32 = jnp.float32

ROWS, COLS, MEMB, LEV = 12, 48, 4, 128
BANDS, BLOCKS = 8, 32
SUB = 8
RUN = COLS // SUB
UNITS = MEMB * RUN
SHARE = UNITS // BANDS
NLAT = ROWS * BANDS
HALF = SHARE * SUB


def lat_partner(band, step):
    hop = step // 2
    away = (2 + hop + hop // 2 + 2 * (hop // 3)) % (BANDS // 2)
    other = (step + hop // 3) % 2
    return (band // 2 + away) % (BANDS // 2) * 2 + (band + other) % 2


def rows_at(start, count=SUB):
    return pl.ds(pl.multiple_of(start, SUB), count)


def wide(row, rows=SUB):
    return jnp.broadcast_to(row, (rows, LEV))


def sublane_sums(vals):
    sub = lax.broadcasted_iota(jnp.int32, (SUB, LEV), 0)
    low = sub < 4
    four = [
        jnp.where(low, vals[k], vals[k + 4]) + pltpu.roll(jnp.where(low, vals[k + 4], vals[k]), 4, 0)
        for k in range(4)
    ]
    low = sub % 4 < 2
    two = [
        jnp.where(low, four[k] + pltpu.roll(four[k], 6, 0), four[k + 2] + pltpu.roll(four[k + 2], 2, 0))
        for k in range(2)
    ]
    low = sub % 2 < 1
    return jnp.where(low, two[0] + pltpu.roll(two[0], 7, 0), two[1] + pltpu.roll(two[1], 1, 0))


def sums_before(val):
    sub = lax.broadcasted_iota(jnp.int32, (SUB, LEV), 0)
    val = jnp.where(sub >= 1, pltpu.roll(val, 1, 0), 0.0)
    for step in (1, 2, 4):
        val = val + jnp.where(sub >= step, pltpu.roll(val, step, 0), 0.0)
    return val


def sums_after(val):
    sub = lax.broadcasted_iota(jnp.int32, (SUB, LEV), 0)
    val = jnp.where(sub < SUB - 1, pltpu.roll(val, SUB - 1, 0), 0.0)
    for step in (1, 2, 4):
        val = val + jnp.where(sub < SUB - step, pltpu.roll(val, SUB - step, 0), 0.0)
    return val


def kernel(
    e_hbm, g_hbm, norm_hbm, lon_hbm, lat_hbm, diag_hbm, below_hbm, out_hbm,
    e_v, g_v, norm_ref, lon_ref, lat_ref, diag_ref, below_ref, out_v, y_v,
    tmp, rk_t, phi_t, w1_t, n_t, phin_t, w1n_t,
    w1n_e, phin_e, w1_e, phi_e,
    lat_pad, lat_rk, lat_rows, lat_t, w1l_e, phil_e, cw1_e, cphi_e,
    vinv,
    cs_a, cr_a, ss_a, sr_a, ts_a, tr_a, rows_a, inv_a,
    cs_b, cr_b, ss_b, sr_b, ts_b, tr_b, rows_b, tb_b, el_b,
    load_sem, store_sem,
    ca_send, ca_recv, sa_send, sa_recv, ta_send, ta_recv,
    cb_send, cb_recv, sb_send, sb_recv, tb_send, tb_recv,
):
    band = lax.axis_index("lat")
    me = lax.axis_index("lon")
    is_solver = me < ROWS
    my_row = me % ROWS

    pairs = (
        (lon_hbm, lon_ref), (norm_hbm, norm_ref), (lat_hbm, lat_ref), (g_hbm, g_v), (e_hbm, e_v),
        (diag_hbm, diag_ref), (below_hbm, below_ref),
    )
    loads = [pltpu.make_async_copy(*pair, load_sem.at[k]) for k, pair in enumerate(pairs)]
    for copy in loads:
        copy.start()

    barrier = pltpu.get_barrier_semaphore()

    def greet_lon(step, _):
        pl.semaphore_signal(barrier, inc=1, device_id=(band, (me + step) % BLOCKS), device_id_type=MESH)
        return 0

    def greet_lat(step, _):
        pl.semaphore_signal(barrier, inc=1, device_id=((band + step) % BANDS, me), device_id_type=MESH)
        return 0

    @pl.when(is_solver)
    def _():
        lax.fori_loop(1, BLOCKS, greet_lon, 0)

    lax.fori_loop(1, BANDS, greet_lat, 0)

    tmp[...] = jnp.full((LEV, LEV), 2048.0, F32)
    loads[0].wait()
    loads[1].wait()
    tmp[0:ROWS, 0:COLS] = lon_ref[...]
    rk_t[...] = 1.0 / tmp[...].T[0:COLS]
    tmp[0:ROWS, 0:COLS] = norm_ref[...]
    n_t[...] = tmp[...].T[0:COLS]
    flow_p = jnp.zeros((1, LEV), F32)
    flow_s = jnp.zeros((1, LEV), F32)
    val_p = rk_t[0:1]
    val_s = rk_t[COLS - 1 : COLS]
    phi_t[0:1] = jnp.zeros((1, LEV), F32)
    phi_t[1:2] = val_p
    w1_t[COLS - 1 : COLS] = val_s
    for i in range(1, COLS):
        flow_p = flow_p + val_p
        val_p = val_p + (1.0 + flow_p) * rk_t[i : i + 1]
        if i < COLS - 1:
            phi_t[i + 1 : i + 2] = val_p
        k = COLS - i
        flow_s = flow_s + val_s
        val_s = val_s + (1.0 + flow_s) * rk_t[k - 1 : k]
        w1_t[k - 1 : k] = val_s
    edge = 1.0 / val_p
    scale = 1.0 / val_s
    cs_a[...] = jnp.zeros((SUB, LEV), F32)
    cs_a[0:1] = edge
    cs_a[1:2] = 1.0 + flow_s * scale
    cs_a[2:3] = flow_p * edge
    w1_t[...] = w1_t[...] * scale
    w1n_t[...] = w1_t[...] * n_t[...]
    phin_t[...] = phi_t[...] * n_t[...]

    @pl.when(is_solver)
    def _():
        pl.semaphore_wait(barrier, ROWS + BANDS - 2)

    @pl.when(jnp.logical_not(is_solver))
    def _():
        pl.semaphore_wait(barrier, ROWS + BANDS - 1)

    def coeff_copy_a(row):
        return pltpu.make_async_remote_copy(
            src_ref=cs_a,
            dst_ref=cr_a.at[rows_at(me * SUB)],
            send_sem=ca_send.at[row],
            recv_sem=ca_recv,
            device_id=(band, row),
            device_id_type=MESH,
        )

    def rhs_copy_a(row):
        return pltpu.make_async_remote_copy(
            src_ref=ss_a.at[rows_at(row * SUB)],
            dst_ref=sr_a.at[rows_at(me * SUB)],
            send_sem=sa_send.at[row],
            recv_sem=sa_recv,
            device_id=(band, row),
            device_id_type=MESH,
        )

    def back_copy_a(target):
        return pltpu.make_async_remote_copy(
            src_ref=ts_a.at[rows_at(target * SUB)],
            dst_ref=tr_a.at[rows_at(my_row * SUB)],
            send_sem=ta_send.at[target],
            recv_sem=ta_recv.at[my_row],
            device_id=(band, target),
            device_id_type=MESH,
        )

    def copy_b(kind, target):
        size = SUB if kind == 0 else 2 * HALF
        source = (cs_b, ss_b, ts_b)[kind]
        dest = (cr_b, sr_b, tr_b)[kind]
        return pltpu.make_async_remote_copy(
            src_ref=source if kind == 0 else source.at[rows_at(target * size, size)],
            dst_ref=dest.at[rows_at(band * size, size)],
            send_sem=(cb_send, sb_send, tb_send)[kind].at[target],
            recv_sem=(cb_recv, sb_recv, tb_recv)[kind].at[band],
            device_id=(target, me),
            device_id_type=MESH,
        )

    def landed_b(kind, source):
        size = SUB if kind == 0 else 2 * HALF
        dest = (cr_b, sr_b, tr_b)[kind]
        slot = dest.at[rows_at(source * size, size)]
        return pltpu.make_async_copy(slot, slot, (cb_recv, sb_recv, tb_recv)[kind].at[source])

    def send_coeff_a(step, _):
        row = (me + step) % ROWS

        @pl.when(row != me)
        def _():
            coeff_copy_a(row).start()

        return 0

    lax.fori_loop(0, ROWS, send_coeff_a, 0)

    @pl.when(is_solver)
    def _():
        cr_a[rows_at(me * SUB)] = cs_a[...]

    lat_pad[...] = jnp.full((16, LEV), 512.0, F32)
    loads[2].wait()
    lat_pad[0:ROWS, 0:COLS] = lat_ref[...]
    lat_rk[...] = 1.0 / lat_pad[...]
    at = band * ROWS + lax.broadcasted_iota(jnp.int32, (16, LEV), 0)
    at = jnp.minimum(at, NLAT - 1 - at).astype(F32)
    angle = (at + 0.5) * (math.pi / NLAT)
    square = angle * angle
    series = jnp.full((16, LEV), 1.0 / math.factorial(13), F32)
    for power in (11, 9, 7, 5, 3, 1):
        series = 1.0 / math.factorial(power) - series * square
    lat_t[0:16] = angle * series

    def cosine(j):
        return lat_t[j : j + 1]

    last = jnp.where(band == BANDS - 1, 0.0, 1.0) * lat_pad[ROWS - 1 : ROWS]
    lat_rows[...] = jnp.zeros((LEV, LEV), F32)
    flow_p = jnp.zeros((1, LEV), F32)
    flow_s = jnp.zeros((1, LEV), F32)
    val_p = lat_rk[0:1]
    val_s = jnp.ones((1, LEV), F32)
    lat_rows[17:18] = val_p
    lat_rows[ROWS - 1 : ROWS] = val_s
    for j in range(1, ROWS):
        flow_p = flow_p + cosine(j) * val_p
        if j < ROWS - 1:
            val_p = val_p + (1.0 + flow_p) * lat_rk[j : j + 1]
            lat_rows[17 + j : 18 + j] = val_p
        k = ROWS - j
        flow_s = flow_s + cosine(k) * val_s
        val_s = val_s + (last + flow_s) * lat_rk[k - 1 : k]
        lat_rows[k - 1 : k] = val_s
    edge = last / (last * val_p + 1.0 + flow_p)
    scale = 1.0 / val_s
    cs_b[...] = jnp.zeros((SUB, LEV), F32)
    cs_b[0:1] = edge
    cs_b[1:2] = cosine(0) + flow_s * scale
    cs_b[2:3] = flow_p * edge
    lat_rows[0:16] = lat_rows[0:16] * scale
    lat_rows[32:48] = lat_rows[0:16] * lat_t[0:16]
    lat_rows[48:64] = lat_rows[16:32] * lat_t[0:16]

    def send_coeff_b(step, _):
        copy_b(0, (band + step) % BANDS).start()
        return 0

    lax.fori_loop(1, BANDS, send_coeff_b, 0)
    cr_b[rows_at(band * SUB)] = cs_b[...]

    for t in range(RUN):
        for source, target in ((w1n_t, w1n_e), (phin_t, phin_e)):
            part = source[pl.ds(t, SUB, stride=RUN), :]
            for j in range(ROWS):
                at = j * COLS + t * SUB
                target[at : at + SUB] = jnp.broadcast_to(part[:, j : j + 1], (SUB, LEV))

    loads[3].wait()
    loads[4].wait()

    def contribute(step, _):
        row = (me + step) % ROWS
        sums = [jnp.zeros((SUB, LEV), F32) for _ in range(2 * MEMB)]
        for t in range(RUN):
            grad = g_v[pl.ds(row * COLS + t, SUB, stride=RUN), :]
            first = w1n_e[rows_at(row * COLS + t * SUB)] * grad
            second = phin_e[rows_at(row * COLS + t * SUB)] * grad
            for m in range(MEMB):
                value = e_v[pl.ds(row * COLS * MEMB + t * MEMB + m, SUB, stride=RUN * MEMB), :]
                sums[m] = sums[m] + first * value
                sums[MEMB + m] = sums[MEMB + m] + second * value
        ss_a[rows_at(row * SUB)] = sublane_sums(sums)

        @pl.when(row != me)
        def _():
            rhs_copy_a(row).start()

        return 0

    lax.fori_loop(0, ROWS, contribute, 0)

    @pl.when(is_solver)
    def _():
        sr_a[rows_at(me * SUB)] = ss_a[rows_at(my_row * SUB)]

    loads[5].wait()
    loads[6].wait()
    tmp[0:SUB] = jnp.zeros((SUB, LEV), F32)
    tmp[0:1, 0 : LEV - 1] = below_ref[...]
    dinv = 1.0 / wide(diag_ref[...])
    lane = lax.broadcasted_iota(jnp.int32, (SUB, LEV), 1)
    ratio = jnp.where(lane == 0, 0.0, -pltpu.roll(wide(tmp[0:1]), 1, 1) * dinv)
    row_ids = lax.broadcasted_iota(jnp.int32, (LEV, LEV), 0)
    col_ids = lax.broadcasted_iota(jnp.int32, (LEV, LEV), 1)
    half = jnp.where(row_ids == col_ids, wide(dinv[0:1], LEV), 0.0)
    step = 1
    while step < LEV:
        half = half + wide(ratio[0:1], LEV) * pltpu.roll(half, step, 1)
        ratio = ratio * pltpu.roll(ratio, step, 1)
        step *= 2
    vinv[...] = lax.dot_general(
        half, half, (((1,), (1,)), ((), ())), precision=HIGHEST, preferred_element_type=F32
    )

    for t in range(RUN):
        for source, target in ((w1_t, w1_e), (phi_t, phi_e)):
            part = source[pl.ds(t, SUB, stride=RUN), :]
            for j in range(ROWS):
                at = j * COLS + t * SUB
                target[at : at + SUB] = jnp.broadcast_to(part[:, j : j + 1], (SUB, LEV))

    def interior(row, _):
        firsts, seconds = [], []
        for t in range(RUN):
            grad = g_v[pl.ds(row * COLS + t, SUB, stride=RUN), :]
            firsts.append(w1n_e[rows_at(row * COLS + t * SUB)] * grad)
            seconds.append(phin_e[rows_at(row * COLS + t * SUB)] * grad)
        for m in range(MEMB):
            values = [
                e_v[pl.ds(row * COLS * MEMB + t * MEMB + m, SUB, stride=RUN * MEMB), :] for t in range(RUN)
            ]
            ahead = [seconds[0] * values[0]]
            for t in range(1, RUN):
                ahead.append(ahead[-1] + seconds[t] * values[t])
            behind = [None] * RUN
            total = jnp.zeros((SUB, LEV), F32)
            for t in reversed(range(RUN)):
                behind[t] = total
                total = total + firsts[t] * values[t]
            before = sums_before(ahead[-1])
            after = sums_after(total)
            for t in range(RUN):
                w1 = w1_e[rows_at(row * COLS + t * SUB)]
                phi = phi_e[rows_at(row * COLS + t * SUB)]
                y_v[rows_at(((m * RUN + t) * ROWS + row) * SUB)] = w1 * (before + ahead[t]) + phi * (
                    after + behind[t]
                )
        return 0

    lax.fori_loop(0, ROWS, interior, 0)

    size = UNITS * SUB

    def vertical(part, _):
        at = rows_at(part * size, size)
        y_v[at] = jnp.dot(y_v[at], vinv[...], precision=HIGHEST, preferred_element_type=F32)
        return 0

    lax.fori_loop(0, ROWS, vertical, 0)

    lat_t[...] = lat_rows[...].T
    for t in range(RUN):
        part = lat_t[pl.ds(t, SUB, stride=RUN), :]
        for number, target in enumerate((w1l_e, phil_e, cw1_e, cphi_e)):
            for j in range(ROWS):
                at = j * COLS + t * SUB
                lane_at = number * 16 + j
                target[at : at + SUB] = jnp.broadcast_to(part[:, lane_at : lane_at + 1], (SUB, LEV))

    def wait_coeff_b(step, _):
        landed_b(0, (band + step) % BANDS).wait()
        return 0

    lax.fori_loop(1, BANDS, wait_coeff_b, 0)
    flow_p = jnp.zeros((1, LEV), F32)
    flow_s = jnp.zeros((1, LEV), F32)
    val_p = jnp.ones((1, LEV), F32)
    val_s = jnp.ones((1, LEV), F32)

    def band_base(p):
        own = cr_b[p * SUB + 1 : p * SUB + 2]
        return own if p == 0 else own + cr_b[(p - 1) * SUB + 2 : (p - 1) * SUB + 3]

    def band_link(p):
        return cr_b[p * SUB : p * SUB + 1]

    rows_b[...] = jnp.zeros((LEV, LEV), F32)
    rows_b[0:1] = val_p
    rows_b[2 * BANDS - 1 : 2 * BANDS] = val_s
    for p in range(BANDS - 1):
        flow_p = flow_p + band_base(p) * val_p
        val_p = val_p + flow_p / band_link(p)
        rows_b[p + 1 : p + 2] = val_p
        k = BANDS - 1 - p
        flow_s = flow_s + band_base(k) * val_s
        val_s = val_s + flow_s / band_link(k - 1)
        rows_b[BANDS + k - 1 : BANDS + k] = val_s
    flow_s = flow_s + band_base(0) * val_s
    rows_b[BANDS : 2 * BANDS] = rows_b[BANDS : 2 * BANDS] * (1.0 / flow_s)
    for p in range(BANDS - 1):
        rows_b[2 * BANDS + p : 2 * BANDS + p + 1] = band_link(p)
    tb_b[...] = rows_b[...].T
    for tt in range(SHARE):
        part = tb_b[pl.ds((band % 2) * SHARE + tt, SUB, stride=RUN), :]
        for number in range(3 * BANDS):
            at = (number * SHARE + tt) * SUB
            el_b[at : at + SUB] = jnp.broadcast_to(part[:, number : number + 1], (SUB, LEV))

    @pl.when(is_solver)
    def _():
        slots = cr_a.at[rows_at(0, (BLOCKS - 1) * SUB)]
        pltpu.make_async_copy(slots, slots, ca_recv).wait()
        link = cr_a[pl.ds(0, BLOCKS, stride=SUB), :]
        base = cr_a[pl.ds(1, BLOCKS, stride=SUB), :] + pltpu.roll(cr_a[pl.ds(2, BLOCKS, stride=SUB), :], 1, 0)
        rows_a[0:BLOCKS] = 1.0 / link
        rows_a[BLOCKS : 2 * BLOCKS] = base
        flow_p = jnp.zeros((1, LEV), F32)
        flow_s = jnp.zeros((1, LEV), F32)
        val_p = rows_a[0:1]
        val_s = rows_a[BLOCKS - 1 : BLOCKS]
        tmp[0:1] = jnp.zeros((1, LEV), F32)
        tmp[1:2] = val_p
        tmp[2 * BLOCKS - 1 : 2 * BLOCKS] = val_s
        for p in range(1, BLOCKS):
            flow_p = flow_p + rows_a[BLOCKS + p : BLOCKS + p + 1] * val_p
            val_p = val_p + (1.0 + flow_p) * rows_a[p : p + 1]
            if p < BLOCKS - 1:
                tmp[p + 1 : p + 2] = val_p
            k = BLOCKS - p
            flow_s = flow_s + rows_a[BLOCKS + k : BLOCKS + k + 1] * val_s
            val_s = val_s + (1.0 + flow_s) * rows_a[k - 1 : k]
            tmp[BLOCKS + k - 1 : BLOCKS + k] = val_s
        first = tmp[BLOCKS : 2 * BLOCKS] * (1.0 / val_s)
        both = first + tmp[0:BLOCKS] * (1.0 / val_p)
        total = jnp.sum(both * base, axis=0, keepdims=True)
        tmp[BLOCKS : 2 * BLOCKS] = first
        tmp[2 * BLOCKS : 3 * BLOCKS] = both * (1.0 / total)
        tmp[3 * BLOCKS : 4 * BLOCKS] = both
        whole = tmp[...]
        lanes = lax.broadcasted_iota(jnp.int32, (LEV, LEV), 1)
        column = jnp.sum(jnp.where(lanes == my_row, whole, 0.0), axis=1, keepdims=True)
        column = jnp.broadcast_to(column, (LEV, LEV))
        tmp[...] = whole.T
        line = wide(tmp[pl.ds(my_row, 1), :])
        phi_row = wide(line[0:1], BLOCKS)
        first_row = wide(pltpu.roll(line, LEV - BLOCKS, 1)[0:1], BLOCKS)
        both_row = wide(pltpu.roll(line, LEV - 2 * BLOCKS, 1)[0:1], BLOCKS)
        sub_ids = lax.broadcasted_iota(jnp.int32, (BLOCKS, LEV), 0)
        lane_ids = lax.broadcasted_iota(jnp.int32, (BLOCKS, LEV), 1)
        inv_a[0:BLOCKS] = (
            jnp.where(
                sub_ids <= lane_ids,
                column[0:BLOCKS] * first_row,
                column[BLOCKS : 2 * BLOCKS] * phi_row,
            )
            + column[3 * BLOCKS : 4 * BLOCKS] * both_row
        )
        link = jnp.sum(jnp.where(lane_ids == my_row, link, 0.0), axis=1, keepdims=True)
        inv_a[BLOCKS : 2 * BLOCKS] = jnp.broadcast_to(link, (BLOCKS, LEV))

    @pl.when(is_solver)
    def _():
        slots = sr_a.at[rows_at(0, (BLOCKS - 1) * SUB)]
        pltpu.make_async_copy(slots, slots, sa_recv).wait()
        link = inv_a[BLOCKS : 2 * BLOCKS]
        inverse = inv_a[0:BLOCKS][:, 0:BLOCKS]
        for m in range(MEMB):
            own = sr_a[pl.ds(m, BLOCKS, stride=SUB), :]
            after = sr_a[pl.ds(MEMB + m, BLOCKS, stride=SUB), :]
            rhs = own + pltpu.roll(link * after, 1, 0)
            rhs = jnp.dot(rhs, vinv[...], precision=HIGHEST, preferred_element_type=F32)
            found = jnp.dot(inverse, rhs, precision=HIGHEST, preferred_element_type=F32)
            ts_a[pl.ds(m, BLOCKS, stride=SUB), :] = found
            ts_a[pl.ds(MEMB + m, BLOCKS, stride=SUB), :] = link * pltpu.roll(found, BLOCKS - 1, 0)

        def send_back(target, _):
            @pl.when(target != me)
            def _():
                back_copy_a(target).start()

            return 0

        lax.fori_loop(0, BLOCKS, send_back, 0)
        tr_a[rows_at(my_row * SUB)] = ts_a[rows_at(me * SUB)]

    def wait_back_a(row, _):
        @pl.when(row != me)
        def _():
            slot = tr_a.at[rows_at(row * SUB)]
            pltpu.make_async_copy(slot, slot, ta_recv.at[row]).wait()

        return 0

    lax.fori_loop(0, ROWS, wait_back_a, 0)

    def finish_lon(step, _):
        share = lat_partner(band, step)
        m = share // 2
        for tt in range(SHARE):
            t = (share % 2) * SHARE + tt
            own = jnp.zeros((SUB, LEV), F32)
            after = jnp.zeros((SUB, LEV), F32)
            for j in range(ROWS):
                at = rows_at(((share * SHARE + tt) * ROWS + j) * SUB)
                coeff = rows_at(j * COLS + t * SUB)
                sep_own = wide(tr_a[pl.ds(j * SUB + m, 1), :])
                sep_next = wide(tr_a[pl.ds(j * SUB + MEMB + m, 1), :])
                value = y_v[at] + w1_e[coeff] * sep_own + phi_e[coeff] * sep_next
                y_v[at] = value
                own = own + w1l_e[coeff] * value
                after = after + phil_e[coeff] * value
            ss_b[rows_at(share * 2 * HALF + tt * SUB)] = own
            ss_b[rows_at(share * 2 * HALF + HALF + tt * SUB)] = after

        @pl.when(share != band)
        def _():
            copy_b(1, share).start()

        return 0

    lax.fori_loop(0, BANDS, finish_lon, 0)
    sr_b[rows_at(band * 2 * HALF, 2 * HALF)] = ss_b[rows_at(band * 2 * HALF, 2 * HALF)]

    def interior_lat(unit, _):
        t = unit % RUN
        total = jnp.zeros((SUB, LEV), F32)
        aheads = []
        for j in range(ROWS):
            at = rows_at((unit * ROWS + j) * SUB)
            total = total + phil_e[rows_at(j * COLS + t * SUB)] * y_v[at]
            aheads.append(total)
        total = jnp.zeros((SUB, LEV), F32)
        for j in reversed(range(ROWS)):
            at = rows_at((unit * ROWS + j) * SUB)
            coeff = rows_at(j * COLS + t * SUB)
            value = y_v[at]
            y_v[at] = cw1_e[coeff] * aheads[j] + cphi_e[coeff] * total
            total = total + w1l_e[coeff] * value
        return 0

    lax.fori_loop(0, UNITS, interior_lat, 0)

    def wait_rhs_b(step, _):
        landed_b(1, (band + step) % BANDS).wait()
        return 0

    lax.fori_loop(1, BANDS, wait_rhs_b, 0)

    for tt in range(SHARE):

        def spread(number):
            at = (number * SHARE + tt) * SUB
            return el_b[at : at + SUB]

        rhs = []
        total = jnp.zeros((SUB, LEV), F32)
        aheads = []
        for p in range(BANDS):
            at = p * 2 * HALF + tt * SUB
            value = sr_b[at : at + SUB]
            if p > 0:
                before = at - HALF
                value = value + spread(2 * BANDS + p - 1) * sr_b[before : before + SUB]
            rhs.append(value)
            total = total + spread(p) * value
            aheads.append(total)
        total = jnp.zeros((SUB, LEV), F32)
        found = None
        for p in reversed(range(BANDS)):
            at = p * 2 * HALF + tt * SUB
            if p == BANDS - 1:
                ts_b[at + HALF : at + HALF + SUB] = jnp.zeros((SUB, LEV), F32)
            else:
                ts_b[at + HALF : at + HALF + SUB] = spread(2 * BANDS + p) * found
            found = spread(BANDS + p) * aheads[p] + spread(p) * total
            ts_b[at : at + SUB] = found
            total = total + spread(BANDS + p) * rhs[p]

    def send_back_b(step, _):
        copy_b(2, lat_partner(band, step)).start()
        return 0

    lax.fori_loop(0, BANDS - 1, send_back_b, 0)
    tr_b[rows_at(band * 2 * HALF, 2 * HALF)] = ts_b[rows_at(band * 2 * HALF, 2 * HALF)]

    def finish(step, _):
        share = lat_partner(band, BANDS - 1 - step)

        @pl.when(share != band)
        def _():
            landed_b(2, share).wait()

        m = share // 2
        for tt in range(SHARE):
            t = (share % 2) * SHARE + tt
            sep_own = tr_b[rows_at(share * 2 * HALF + tt * SUB)]
            sep_next = tr_b[rows_at(share * 2 * HALF + HALF + tt * SUB)]
            for j in range(ROWS):
                at = rows_at(((share * SHARE + tt) * ROWS + j) * SUB)
                coeff = rows_at(j * COLS + t * SUB)
                out_v[pl.ds(j * COLS * MEMB + t * MEMB + m, SUB, stride=RUN * MEMB), :] = (
                    y_v[at] + cw1_e[coeff] * sep_own + cphi_e[coeff] * sep_next
                )
        return 0

    lax.fori_loop(0, BANDS, finish, 0)
    result = pltpu.make_async_copy(out_v, out_hbm, store_sem)
    result.start()

    def sent_a(row, _):
        @pl.when(row != me)
        def _():
            coeff_copy_a(row).wait_send()
            rhs_copy_a(row).wait_send()

        return 0

    lax.fori_loop(0, ROWS, sent_a, 0)

    @pl.when(is_solver)
    def _():
        def sent_back(step, _):
            back_copy_a((me + step) % BLOCKS).wait_send()
            return 0

        lax.fori_loop(1, BLOCKS, sent_back, 0)

    def sent_b(step, _):
        for kind in range(3):
            copy_b(kind, (band + step) % BANDS).wait_send()
        return 0

    lax.fori_loop(1, BANDS, sent_b, 0)
    result.wait()


def shards(
    ensemble, grad_increment, normalization, lon_diffusion, lat_diffusion, vert_diag, vert_sub
):
    block = ROWS * COLS * MEMB
    anywhere = pl.BlockSpec(memory_space=pl.ANY)

    def buf(rows):
        return pltpu.VMEM((rows, LEV), F32)

    coeffs = ROWS * COLS
    dma = pltpu.SemaphoreType.DMA
    scratch = [
        buf(block), buf(coeffs), *[pltpu.VMEM((ROWS, COLS), F32)] * 3, buf(1), pltpu.VMEM((1, LEV - 1), F32),
        buf(block), buf(block),
        buf(LEV), *[buf(COLS)] * 6,
        *[buf(coeffs)] * 4,
        buf(16), buf(16), buf(LEV), buf(LEV), *[buf(coeffs)] * 4,
        buf(LEV),
        buf(SUB), buf(BLOCKS * SUB), buf(ROWS * SUB), buf(BLOCKS * SUB), buf(BLOCKS * SUB), buf(ROWS * SUB),
        buf(2 * BLOCKS), buf(2 * BLOCKS),
        buf(SUB), buf(BANDS * SUB), *[buf(BANDS * 2 * HALF)] * 4,
        buf(LEV), buf(LEV), buf(3 * BANDS * HALF),
        dma((7,)), dma,
        dma((ROWS,)), dma, dma((ROWS,)), dma, dma((BLOCKS,)), dma((ROWS,)),
        *[dma((BANDS,))] * 6,
    ]
    out = pl.pallas_call(
        kernel,
        out_shape=jax.ShapeDtypeStruct((block, LEV), F32),
        in_specs=[anywhere] * 7,
        out_specs=anywhere,
        scratch_shapes=scratch,
        compiler_params=pltpu.CompilerParams(
            collective_id=0, has_side_effects=True, vmem_limit_bytes=60 * 1024 * 1024
        ),
    )(
        ensemble.reshape(block, LEV),
        grad_increment.reshape(coeffs, LEV),
        normalization,
        lon_diffusion,
        lat_diffusion,
        vert_diag.reshape(1, LEV),
        vert_sub.reshape(1, LEV - 1),
    )
    return out.reshape(ROWS, COLS, MEMB, LEV)


def solution(mesh):
    in_specs = (
        P("lat", "lon", None, None),
        P("lat", "lon", None),
        P("lat", "lon"),
        P("lat", "lon"),
        P("lat", "lon"),
        P(),
        P(),
    )
    out_specs = P("lat", "lon", None, None)
    return jax.shard_map(shards, mesh=mesh, in_specs=in_specs, out_specs=out_specs, check_vma=False)
```

```python
import functools
import math

import jax
import jax.numpy as jnp
from jax import lax
from jax.experimental import pallas as pl
from jax.experimental.pallas import tpu as pltpu
from jax.sharding import PartitionSpec as P

HIGHEST = lax.Precision.HIGHEST
MESH = pl.DeviceIdType.MESH
F32 = jnp.float32

ROWS, COLS, MEMB, LEV = 12, 48, 4, 128
BANDS, BLOCKS = 8, 32
SUB = 8
RUN = COLS // SUB
UNITS = MEMB * RUN
SHARE = UNITS // BANDS
NLAT = ROWS * BANDS
HALF = SHARE * SUB


def lat_partner(band, step):
    hop = step // 2
    away = (2 + hop + hop // 2 + 2 * (hop // 3)) % (BANDS // 2)
    other = (step + hop // 3) % 2
    return (band // 2 + away) % (BANDS // 2) * 2 + (band + other) % 2


def rows_at(start, count=SUB):
    return pl.ds(pl.multiple_of(start, SUB), count)


def wide(row, rows=SUB):
    return jnp.broadcast_to(row, (rows, LEV))


def sublane_sums(vals):
    sub = lax.broadcasted_iota(jnp.int32, (SUB, LEV), 0)
    low = sub < 4
    four = [
        jnp.where(low, vals[k], vals[k + 4]) + pltpu.roll(jnp.where(low, vals[k + 4], vals[k]), 4, 0)
        for k in range(4)
    ]
    low = sub % 4 < 2
    two = [
        jnp.where(low, four[k] + pltpu.roll(four[k], 6, 0), four[k + 2] + pltpu.roll(four[k + 2], 2, 0))
        for k in range(2)
    ]
    low = sub % 2 < 1
    return jnp.where(low, two[0] + pltpu.roll(two[0], 7, 0), two[1] + pltpu.roll(two[1], 1, 0))


def sums_before(val):
    sub = lax.broadcasted_iota(jnp.int32, (SUB, LEV), 0)
    val = jnp.where(sub >= 1, pltpu.roll(val, 1, 0), 0.0)
    for step in (1, 2, 4):
        val = val + jnp.where(sub >= step, pltpu.roll(val, step, 0), 0.0)
    return val


def sums_after(val):
    sub = lax.broadcasted_iota(jnp.int32, (SUB, LEV), 0)
    val = jnp.where(sub < SUB - 1, pltpu.roll(val, SUB - 1, 0), 0.0)
    for step in (1, 2, 4):
        val = val + jnp.where(sub < SUB - step, pltpu.roll(val, SUB - step, 0), 0.0)
    return val


def kernel(
    e_hbm, g_hbm, norm_hbm, lon_hbm, lat_hbm, diag_hbm, below_hbm, out_v,
    e_v, g_v, norm_ref, lon_ref, lat_ref, diag_ref, below_ref, y_v,
    tmp, rk_t, phi_t, w1_t, n_t, phin_t, w1n_t,
    w1n_e, phin_e, w1_e, phi_e,
    lat_pad, lat_rk, lat_rows, lat_t, w1l_e, phil_e, cw1_e, cphi_e,
    vinv,
    cs_a, cr_a, ss_a, sr_a, ts_a, tr_a, rows_a, inv_a,
    cs_b, cr_b, ss_b, sr_b, ts_b, tr_b, rows_b, tb_b, el_b,
    load_sem,
    ca_send, ca_recv, sa_send, sa_recv, ta_send, ta_recv,
    cb_send, cb_recv, sb_send, sb_recv, tb_send, tb_recv,
):
    band = lax.axis_index("lat")
    me = lax.axis_index("lon")
    is_solver = me < ROWS
    my_row = me % ROWS

    pairs = (
        (lon_hbm, lon_ref), (norm_hbm, norm_ref), (lat_hbm, lat_ref), (g_hbm, g_v), (e_hbm, e_v),
        (diag_hbm, diag_ref), (below_hbm, below_ref),
    )
    loads = [pltpu.make_async_copy(*pair, load_sem.at[k]) for k, pair in enumerate(pairs)]
    for copy in loads:
        copy.start()

    barrier = pltpu.get_barrier_semaphore()

    def greet_lon(step, _):
        pl.semaphore_signal(barrier, inc=1, device_id=(band, (me + step) % BLOCKS), device_id_type=MESH)
        return 0

    def greet_lat(step, _):
        pl.semaphore_signal(barrier, inc=1, device_id=((band + step) % BANDS, me), device_id_type=MESH)
        return 0

    @pl.when(is_solver)
    def _():
        lax.fori_loop(1, BLOCKS, greet_lon, 0)

    lax.fori_loop(1, BANDS, greet_lat, 0)

    tmp[...] = jnp.full((LEV, LEV), 2048.0, F32)
    loads[0].wait()
    loads[1].wait()
    tmp[0:ROWS, 0:COLS] = lon_ref[...]
    rk_t[...] = 1.0 / tmp[...].T[0:COLS]
    tmp[0:ROWS, 0:COLS] = norm_ref[...]
    n_t[...] = tmp[...].T[0:COLS]
    flow_p = jnp.zeros((1, LEV), F32)
    flow_s = jnp.zeros((1, LEV), F32)
    val_p = rk_t[0:1]
    val_s = rk_t[COLS - 1 : COLS]
    phi_t[0:1] = jnp.zeros((1, LEV), F32)
    phi_t[1:2] = val_p
    w1_t[COLS - 1 : COLS] = val_s
    for i in range(1, COLS):
        flow_p = flow_p + val_p
        val_p = val_p + (1.0 + flow_p) * rk_t[i : i + 1]
        if i < COLS - 1:
            phi_t[i + 1 : i + 2] = val_p
        k = COLS - i
        flow_s = flow_s + val_s
        val_s = val_s + (1.0 + flow_s) * rk_t[k - 1 : k]
        w1_t[k - 1 : k] = val_s
    edge = 1.0 / val_p
    scale = 1.0 / val_s
    cs_a[...] = jnp.zeros((SUB, LEV), F32)
    cs_a[0:1] = edge
    cs_a[1:2] = 1.0 + flow_s * scale
    cs_a[2:3] = flow_p * edge
    w1_t[...] = w1_t[...] * scale
    w1n_t[...] = w1_t[...] * n_t[...]
    phin_t[...] = phi_t[...] * n_t[...]

    @pl.when(is_solver)
    def _():
        pl.semaphore_wait(barrier, ROWS + BANDS - 2)

    @pl.when(jnp.logical_not(is_solver))
    def _():
        pl.semaphore_wait(barrier, ROWS + BANDS - 1)

    def coeff_copy_a(row):
        return pltpu.make_async_remote_copy(
            src_ref=cs_a,
            dst_ref=cr_a.at[rows_at(me * SUB)],
            send_sem=ca_send.at[row],
            recv_sem=ca_recv,
            device_id=(band, row),
            device_id_type=MESH,
        )

    def rhs_copy_a(row):
        return pltpu.make_async_remote_copy(
            src_ref=ss_a.at[rows_at(row * SUB)],
            dst_ref=sr_a.at[rows_at(me * SUB)],
            send_sem=sa_send.at[row],
            recv_sem=sa_recv,
            device_id=(band, row),
            device_id_type=MESH,
        )

    def back_copy_a(target):
        return pltpu.make_async_remote_copy(
            src_ref=ts_a.at[rows_at(target * SUB)],
            dst_ref=tr_a.at[rows_at(my_row * SUB)],
            send_sem=ta_send.at[target],
            recv_sem=ta_recv.at[my_row],
            device_id=(band, target),
            device_id_type=MESH,
        )

    def copy_b(kind, target):
        size = SUB if kind == 0 else 2 * HALF
        source = (cs_b, ss_b, ts_b)[kind]
        dest = (cr_b, sr_b, tr_b)[kind]
        return pltpu.make_async_remote_copy(
            src_ref=source if kind == 0 else source.at[rows_at(target * size, size)],
            dst_ref=dest.at[rows_at(band * size, size)],
            send_sem=(cb_send, sb_send, tb_send)[kind].at[target],
            recv_sem=(cb_recv, sb_recv, tb_recv)[kind].at[band],
            device_id=(target, me),
            device_id_type=MESH,
        )

    def landed_b(kind, source):
        size = SUB if kind == 0 else 2 * HALF
        dest = (cr_b, sr_b, tr_b)[kind]
        slot = dest.at[rows_at(source * size, size)]
        return pltpu.make_async_copy(slot, slot, (cb_recv, sb_recv, tb_recv)[kind].at[source])

    def send_coeff_a(step, _):
        row = (me + step) % ROWS

        @pl.when(row != me)
        def _():
            coeff_copy_a(row).start()

        return 0

    lax.fori_loop(0, ROWS, send_coeff_a, 0)

    @pl.when(is_solver)
    def _():
        cr_a[rows_at(me * SUB)] = cs_a[...]

    lat_pad[...] = jnp.full((16, LEV), 512.0, F32)
    loads[2].wait()
    lat_pad[0:ROWS, 0:COLS] = lat_ref[...]
    lat_rk[...] = 1.0 / lat_pad[...]
    at = band * ROWS + lax.broadcasted_iota(jnp.int32, (16, LEV), 0)
    at = jnp.minimum(at, NLAT - 1 - at).astype(F32)
    angle = (at + 0.5) * (math.pi / NLAT)
    square = angle * angle
    series = jnp.full((16, LEV), 1.0 / math.factorial(13), F32)
    for power in (11, 9, 7, 5, 3, 1):
        series = 1.0 / math.factorial(power) - series * square
    lat_t[0:16] = angle * series

    def cosine(j):
        return lat_t[j : j + 1]

    last = jnp.where(band == BANDS - 1, 0.0, 1.0) * lat_pad[ROWS - 1 : ROWS]
    lat_rows[...] = jnp.zeros((LEV, LEV), F32)
    flow_p = jnp.zeros((1, LEV), F32)
    flow_s = jnp.zeros((1, LEV), F32)
    val_p = lat_rk[0:1]
    val_s = jnp.ones((1, LEV), F32)
    lat_rows[17:18] = val_p
    lat_rows[ROWS - 1 : ROWS] = val_s
    for j in range(1, ROWS):
        flow_p = flow_p + cosine(j) * val_p
        if j < ROWS - 1:
            val_p = val_p + (1.0 + flow_p) * lat_rk[j : j + 1]
            lat_rows[17 + j : 18 + j] = val_p
        k = ROWS - j
        flow_s = flow_s + cosine(k) * val_s
        val_s = val_s + (last + flow_s) * lat_rk[k - 1 : k]
        lat_rows[k - 1 : k] = val_s
    edge = last / (last * val_p + 1.0 + flow_p)
    scale = 1.0 / val_s
    cs_b[...] = jnp.zeros((SUB, LEV), F32)
    cs_b[0:1] = edge
    cs_b[1:2] = cosine(0) + flow_s * scale
    cs_b[2:3] = flow_p * edge
    lat_rows[0:16] = lat_rows[0:16] * scale
    lat_rows[32:48] = lat_rows[0:16] * lat_t[0:16]
    lat_rows[48:64] = lat_rows[16:32] * lat_t[0:16]

    def send_coeff_b(step, _):
        copy_b(0, (band + step) % BANDS).start()
        return 0

    lax.fori_loop(1, BANDS, send_coeff_b, 0)
    cr_b[rows_at(band * SUB)] = cs_b[...]

    for t in range(RUN):
        for source, target in ((w1n_t, w1n_e), (phin_t, phin_e)):
            part = source[pl.ds(t, SUB, stride=RUN), :]
            for j in range(ROWS):
                at = j * COLS + t * SUB
                target[at : at + SUB] = jnp.broadcast_to(part[:, j : j + 1], (SUB, LEV))

    loads[3].wait()
    loads[4].wait()

    def contribute(step, _):
        row = (me + step) % ROWS
        sums = [jnp.zeros((SUB, LEV), F32) for _ in range(2 * MEMB)]
        for t in range(RUN):
            grad = g_v[pl.ds(row * COLS + t, SUB, stride=RUN), :]
            first = w1n_e[rows_at(row * COLS + t * SUB)] * grad
            second = phin_e[rows_at(row * COLS + t * SUB)] * grad
            for m in range(MEMB):
                value = e_v[pl.ds(row * COLS * MEMB + t * MEMB + m, SUB, stride=RUN * MEMB), :]
                sums[m] = sums[m] + first * value
                sums[MEMB + m] = sums[MEMB + m] + second * value
        ss_a[rows_at(row * SUB)] = sublane_sums(sums)

        @pl.when(row != me)
        def _():
            rhs_copy_a(row).start()

        return 0

    lax.fori_loop(0, ROWS, contribute, 0)

    @pl.when(is_solver)
    def _():
        sr_a[rows_at(me * SUB)] = ss_a[rows_at(my_row * SUB)]

    loads[5].wait()
    loads[6].wait()
    tmp[0:SUB] = jnp.zeros((SUB, LEV), F32)
    tmp[0:1, 0 : LEV - 1] = below_ref[...]
    dinv = 1.0 / wide(diag_ref[...])
    lane = lax.broadcasted_iota(jnp.int32, (SUB, LEV), 1)
    ratio = jnp.where(lane == 0, 0.0, -pltpu.roll(wide(tmp[0:1]), 1, 1) * dinv)
    row_ids = lax.broadcasted_iota(jnp.int32, (LEV, LEV), 0)
    col_ids = lax.broadcasted_iota(jnp.int32, (LEV, LEV), 1)
    half = jnp.where(row_ids == col_ids, wide(dinv[0:1], LEV), 0.0)
    step = 1
    while step < LEV:
        half = half + wide(ratio[0:1], LEV) * pltpu.roll(half, step, 1)
        ratio = ratio * pltpu.roll(ratio, step, 1)
        step *= 2
    vinv[...] = lax.dot_general(
        half, half, (((1,), (1,)), ((), ())), precision=HIGHEST, preferred_element_type=F32
    )

    for t in range(RUN):
        for source, target in ((w1_t, w1_e), (phi_t, phi_e)):
            part = source[pl.ds(t, SUB, stride=RUN), :]
            for j in range(ROWS):
                at = j * COLS + t * SUB
                target[at : at + SUB] = jnp.broadcast_to(part[:, j : j + 1], (SUB, LEV))

    def interior(row, _):
        firsts, seconds = [], []
        for t in range(RUN):
            grad = g_v[pl.ds(row * COLS + t, SUB, stride=RUN), :]
            firsts.append(w1n_e[rows_at(row * COLS + t * SUB)] * grad)
            seconds.append(phin_e[rows_at(row * COLS + t * SUB)] * grad)
        for m in range(MEMB):
            values = [
                e_v[pl.ds(row * COLS * MEMB + t * MEMB + m, SUB, stride=RUN * MEMB), :] for t in range(RUN)
            ]
            ahead = [seconds[0] * values[0]]
            for t in range(1, RUN):
                ahead.append(ahead[-1] + seconds[t] * values[t])
            behind = [None] * RUN
            total = jnp.zeros((SUB, LEV), F32)
            for t in reversed(range(RUN)):
                behind[t] = total
                total = total + firsts[t] * values[t]
            before = sums_before(ahead[-1])
            after = sums_after(total)
            for t in range(RUN):
                w1 = w1_e[rows_at(row * COLS + t * SUB)]
                phi = phi_e[rows_at(row * COLS + t * SUB)]
                y_v[rows_at(((m * RUN + t) * ROWS + row) * SUB)] = w1 * (before + ahead[t]) + phi * (
                    after + behind[t]
                )
        return 0

    lax.fori_loop(0, ROWS, interior, 0)

    size = UNITS * SUB

    def vertical(part, _):
        at = rows_at(part * size, size)
        y_v[at] = jnp.dot(y_v[at], vinv[...], precision=HIGHEST, preferred_element_type=F32)
        return 0

    lax.fori_loop(0, ROWS, vertical, 0)

    lat_t[...] = lat_rows[...].T
    for t in range(RUN):
        part = lat_t[pl.ds(t, SUB, stride=RUN), :]
        for number, target in enumerate((w1l_e, phil_e, cw1_e, cphi_e)):
            for j in range(ROWS):
                at = j * COLS + t * SUB
                lane_at = number * 16 + j
                target[at : at + SUB] = jnp.broadcast_to(part[:, lane_at : lane_at + 1], (SUB, LEV))

    def wait_coeff_b(step, _):
        landed_b(0, (band + step) % BANDS).wait()
        return 0

    lax.fori_loop(1, BANDS, wait_coeff_b, 0)
    flow_p = jnp.zeros((1, LEV), F32)
    flow_s = jnp.zeros((1, LEV), F32)
    val_p = jnp.ones((1, LEV), F32)
    val_s = jnp.ones((1, LEV), F32)

    def band_base(p):
        own = cr_b[p * SUB + 1 : p * SUB + 2]
        return own if p == 0 else own + cr_b[(p - 1) * SUB + 2 : (p - 1) * SUB + 3]

    def band_link(p):
        return cr_b[p * SUB : p * SUB + 1]

    rows_b[...] = jnp.zeros((LEV, LEV), F32)
    rows_b[0:1] = val_p
    rows_b[2 * BANDS - 1 : 2 * BANDS] = val_s
    for p in range(BANDS - 1):
        flow_p = flow_p + band_base(p) * val_p
        val_p = val_p + flow_p / band_link(p)
        rows_b[p + 1 : p + 2] = val_p
        k = BANDS - 1 - p
        flow_s = flow_s + band_base(k) * val_s
        val_s = val_s + flow_s / band_link(k - 1)
        rows_b[BANDS + k - 1 : BANDS + k] = val_s
    flow_s = flow_s + band_base(0) * val_s
    rows_b[BANDS : 2 * BANDS] = rows_b[BANDS : 2 * BANDS] * (1.0 / flow_s)
    for p in range(BANDS - 1):
        rows_b[2 * BANDS + p : 2 * BANDS + p + 1] = band_link(p)
    tb_b[...] = rows_b[...].T
    for tt in range(SHARE):
        part = tb_b[pl.ds((band % 2) * SHARE + tt, SUB, stride=RUN), :]
        for number in range(3 * BANDS):
            at = (number * SHARE + tt) * SUB
            el_b[at : at + SUB] = jnp.broadcast_to(part[:, number : number + 1], (SUB, LEV))

    @pl.when(is_solver)
    def _():
        slots = cr_a.at[rows_at(0, (BLOCKS - 1) * SUB)]
        pltpu.make_async_copy(slots, slots, ca_recv).wait()
        link = cr_a[pl.ds(0, BLOCKS, stride=SUB), :]
        base = cr_a[pl.ds(1, BLOCKS, stride=SUB), :] + pltpu.roll(cr_a[pl.ds(2, BLOCKS, stride=SUB), :], 1, 0)
        rows_a[0:BLOCKS] = 1.0 / link
        rows_a[BLOCKS : 2 * BLOCKS] = base
        flow_p = jnp.zeros((1, LEV), F32)
        flow_s = jnp.zeros((1, LEV), F32)
        val_p = rows_a[0:1]
        val_s = rows_a[BLOCKS - 1 : BLOCKS]
        tmp[0:1] = jnp.zeros((1, LEV), F32)
        tmp[1:2] = val_p
        tmp[2 * BLOCKS - 1 : 2 * BLOCKS] = val_s
        for p in range(1, BLOCKS):
            flow_p = flow_p + rows_a[BLOCKS + p : BLOCKS + p + 1] * val_p
            val_p = val_p + (1.0 + flow_p) * rows_a[p : p + 1]
            if p < BLOCKS - 1:
                tmp[p + 1 : p + 2] = val_p
            k = BLOCKS - p
            flow_s = flow_s + rows_a[BLOCKS + k : BLOCKS + k + 1] * val_s
            val_s = val_s + (1.0 + flow_s) * rows_a[k - 1 : k]
            tmp[BLOCKS + k - 1 : BLOCKS + k] = val_s
        first = tmp[BLOCKS : 2 * BLOCKS] * (1.0 / val_s)
        both = first + tmp[0:BLOCKS] * (1.0 / val_p)
        total = jnp.sum(both * base, axis=0, keepdims=True)
        tmp[BLOCKS : 2 * BLOCKS] = first
        tmp[2 * BLOCKS : 3 * BLOCKS] = both * (1.0 / total)
        tmp[3 * BLOCKS : 4 * BLOCKS] = both
        whole = tmp[...]
        lanes = lax.broadcasted_iota(jnp.int32, (LEV, LEV), 1)
        column = jnp.sum(jnp.where(lanes == my_row, whole, 0.0), axis=1, keepdims=True)
        column = jnp.broadcast_to(column, (LEV, LEV))
        tmp[...] = whole.T
        line = wide(tmp[pl.ds(my_row, 1), :])
        phi_row = wide(line[0:1], BLOCKS)
        first_row = wide(pltpu.roll(line, LEV - BLOCKS, 1)[0:1], BLOCKS)
        both_row = wide(pltpu.roll(line, LEV - 2 * BLOCKS, 1)[0:1], BLOCKS)
        sub_ids = lax.broadcasted_iota(jnp.int32, (BLOCKS, LEV), 0)
        lane_ids = lax.broadcasted_iota(jnp.int32, (BLOCKS, LEV), 1)
        inv_a[0:BLOCKS] = (
            jnp.where(
                sub_ids <= lane_ids,
                column[0:BLOCKS] * first_row,
                column[BLOCKS : 2 * BLOCKS] * phi_row,
            )
            + column[3 * BLOCKS : 4 * BLOCKS] * both_row
        )
        link = jnp.sum(jnp.where(lane_ids == my_row, link, 0.0), axis=1, keepdims=True)
        inv_a[BLOCKS : 2 * BLOCKS] = jnp.broadcast_to(link, (BLOCKS, LEV))

    @pl.when(is_solver)
    def _():
        slots = sr_a.at[rows_at(0, (BLOCKS - 1) * SUB)]
        pltpu.make_async_copy(slots, slots, sa_recv).wait()
        link = inv_a[BLOCKS : 2 * BLOCKS]
        inverse = inv_a[0:BLOCKS][:, 0:BLOCKS]
        for m in range(MEMB):
            own = sr_a[pl.ds(m, BLOCKS, stride=SUB), :]
            after = sr_a[pl.ds(MEMB + m, BLOCKS, stride=SUB), :]
            rhs = own + pltpu.roll(link * after, 1, 0)
            rhs = jnp.dot(rhs, vinv[...], precision=HIGHEST, preferred_element_type=F32)
            found = jnp.dot(inverse, rhs, precision=HIGHEST, preferred_element_type=F32)
            ts_a[pl.ds(m, BLOCKS, stride=SUB), :] = found
            ts_a[pl.ds(MEMB + m, BLOCKS, stride=SUB), :] = link * pltpu.roll(found, BLOCKS - 1, 0)

        def send_back(target, _):
            @pl.when(target != me)
            def _():
                back_copy_a(target).start()

            return 0

        lax.fori_loop(0, BLOCKS, send_back, 0)
        tr_a[rows_at(my_row * SUB)] = ts_a[rows_at(me * SUB)]

    def wait_back_a(row, _):
        @pl.when(row != me)
        def _():
            slot = tr_a.at[rows_at(row * SUB)]
            pltpu.make_async_copy(slot, slot, ta_recv.at[row]).wait()

        return 0

    lax.fori_loop(0, ROWS, wait_back_a, 0)

    def finish_lon(step, _):
        share = lat_partner(band, step)
        m = share // 2
        for tt in range(SHARE):
            t = (share % 2) * SHARE + tt
            own = jnp.zeros((SUB, LEV), F32)
            after = jnp.zeros((SUB, LEV), F32)
            for j in range(ROWS):
                at = rows_at(((share * SHARE + tt) * ROWS + j) * SUB)
                coeff = rows_at(j * COLS + t * SUB)
                sep_own = wide(tr_a[pl.ds(j * SUB + m, 1), :])
                sep_next = wide(tr_a[pl.ds(j * SUB + MEMB + m, 1), :])
                value = y_v[at] + w1_e[coeff] * sep_own + phi_e[coeff] * sep_next
                y_v[at] = value
                own = own + w1l_e[coeff] * value
                after = after + phil_e[coeff] * value
            ss_b[rows_at(share * 2 * HALF + tt * SUB)] = own
            ss_b[rows_at(share * 2 * HALF + HALF + tt * SUB)] = after

        @pl.when(share != band)
        def _():
            copy_b(1, share).start()

        return 0

    lax.fori_loop(0, BANDS, finish_lon, 0)
    sr_b[rows_at(band * 2 * HALF, 2 * HALF)] = ss_b[rows_at(band * 2 * HALF, 2 * HALF)]

    def interior_lat(unit, _):
        t = unit % RUN
        total = jnp.zeros((SUB, LEV), F32)
        aheads = []
        for j in range(ROWS):
            at = rows_at((unit * ROWS + j) * SUB)
            total = total + phil_e[rows_at(j * COLS + t * SUB)] * y_v[at]
            aheads.append(total)
        total = jnp.zeros((SUB, LEV), F32)
        for j in reversed(range(ROWS)):
            at = rows_at((unit * ROWS + j) * SUB)
            coeff = rows_at(j * COLS + t * SUB)
            value = y_v[at]
            y_v[at] = cw1_e[coeff] * aheads[j] + cphi_e[coeff] * total
            total = total + w1l_e[coeff] * value
        return 0

    lax.fori_loop(0, UNITS, interior_lat, 0)

    def wait_rhs_b(step, _):
        landed_b(1, (band + step) % BANDS).wait()
        return 0

    lax.fori_loop(1, BANDS, wait_rhs_b, 0)

    for tt in range(SHARE):

        def spread(number):
            at = (number * SHARE + tt) * SUB
            return el_b[at : at + SUB]

        rhs = []
        total = jnp.zeros((SUB, LEV), F32)
        aheads = []
        for p in range(BANDS):
            at = p * 2 * HALF + tt * SUB
            value = sr_b[at : at + SUB]
            if p > 0:
                before = at - HALF
                value = value + spread(2 * BANDS + p - 1) * sr_b[before : before + SUB]
            rhs.append(value)
            total = total + spread(p) * value
            aheads.append(total)
        total = jnp.zeros((SUB, LEV), F32)
        found = None
        for p in reversed(range(BANDS)):
            at = p * 2 * HALF + tt * SUB
            if p == BANDS - 1:
                ts_b[at + HALF : at + HALF + SUB] = jnp.zeros((SUB, LEV), F32)
            else:
                ts_b[at + HALF : at + HALF + SUB] = spread(2 * BANDS + p) * found
            found = spread(BANDS + p) * aheads[p] + spread(p) * total
            ts_b[at : at + SUB] = found
            total = total + spread(BANDS + p) * rhs[p]

    def send_back_b(step, _):
        copy_b(2, lat_partner(band, step)).start()
        return 0

    lax.fori_loop(0, BANDS - 1, send_back_b, 0)
    tr_b[rows_at(band * 2 * HALF, 2 * HALF)] = ts_b[rows_at(band * 2 * HALF, 2 * HALF)]

    def sent_a(row, _):
        @pl.when(row != me)
        def _():
            coeff_copy_a(row).wait_send()
            rhs_copy_a(row).wait_send()

        return 0

    lax.fori_loop(0, ROWS, sent_a, 0)

    @pl.when(is_solver)
    def _():
        def sent_back(step, _):
            back_copy_a((me + step) % BLOCKS).wait_send()
            return 0

        lax.fori_loop(1, BLOCKS, sent_back, 0)

    def sent_b(step, _):
        for kind in range(3):
            copy_b(kind, (band + step) % BANDS).wait_send()
        return 0

    lax.fori_loop(1, BANDS, sent_b, 0)

    def finish(step, _):
        share = lat_partner(band, BANDS - 1 - step)

        @pl.when(share != band)
        def _():
            landed_b(2, share).wait()

        m = share // 2
        for tt in range(SHARE):
            t = (share % 2) * SHARE + tt
            sep_own = tr_b[rows_at(share * 2 * HALF + tt * SUB)]
            sep_next = tr_b[rows_at(share * 2 * HALF + HALF + tt * SUB)]
            for j in range(ROWS):
                at = rows_at(((share * SHARE + tt) * ROWS + j) * SUB)
                coeff = rows_at(j * COLS + t * SUB)
                out_v[pl.ds(j * COLS * MEMB + t * MEMB + m, SUB, stride=RUN * MEMB), :] = (
                    y_v[at] + cw1_e[coeff] * sep_own + cphi_e[coeff] * sep_next
                )
        return 0

    lax.fori_loop(0, BANDS, finish, 0)


def shards(
    ensemble, grad_increment, normalization, lon_diffusion, lat_diffusion, vert_diag, vert_sub
):
    block = ROWS * COLS * MEMB
    anywhere = pl.BlockSpec(memory_space=pl.ANY)

    def buf(rows):
        return pltpu.VMEM((rows, LEV), F32)

    coeffs = ROWS * COLS
    dma = pltpu.SemaphoreType.DMA
    scratch = [
        buf(block), buf(coeffs), *[pltpu.VMEM((ROWS, COLS), F32)] * 3, buf(1), pltpu.VMEM((1, LEV - 1), F32),
        buf(block),
        buf(LEV), *[buf(COLS)] * 6,
        *[buf(coeffs)] * 4,
        buf(16), buf(16), buf(LEV), buf(LEV), *[buf(coeffs)] * 4,
        buf(LEV),
        buf(SUB), buf(BLOCKS * SUB), buf(ROWS * SUB), buf(BLOCKS * SUB), buf(BLOCKS * SUB), buf(ROWS * SUB),
        buf(2 * BLOCKS), buf(2 * BLOCKS),
        buf(SUB), buf(BANDS * SUB), *[buf(BANDS * 2 * HALF)] * 4,
        buf(LEV), buf(LEV), buf(3 * BANDS * HALF),
        dma((7,)),
        dma((ROWS,)), dma, dma((ROWS,)), dma, dma((BLOCKS,)), dma((ROWS,)),
        *[dma((BANDS,))] * 6,
    ]
    out = pl.pallas_call(
        kernel,
        out_shape=pltpu.VMEM((block, LEV), F32),
        in_specs=[anywhere] * 7,
        out_specs=pl.BlockSpec(memory_space=pltpu.VMEM),
        scratch_shapes=scratch,
        compiler_params=pltpu.CompilerParams(
            collective_id=0, has_side_effects=True, vmem_limit_bytes=60 * 1024 * 1024
        ),
    )(
        ensemble.reshape(block, LEV),
        grad_increment.reshape(coeffs, LEV),
        normalization,
        lon_diffusion,
        lat_diffusion,
        vert_diag.reshape(1, LEV),
        vert_sub.reshape(1, LEV - 1),
    )
    return out.reshape(ROWS, COLS, MEMB, LEV)


def solution(mesh):
    in_specs = (
        P("lat", "lon", None, None),
        P("lat", "lon", None),
        P("lat", "lon"),
        P("lat", "lon"),
        P("lat", "lon"),
        P(),
        P(),
    )
    out_specs = P("lat", "lon", None, None)
    return jax.shard_map(shards, mesh=mesh, in_specs=in_specs, out_specs=out_specs, check_vma=False)
```

```python
import functools
import math

import jax
import jax.numpy as jnp
from jax import lax
from jax.experimental import pallas as pl
from jax.experimental.pallas import tpu as pltpu
from jax.sharding import PartitionSpec as P

HIGHEST = lax.Precision.HIGHEST
MESH = pl.DeviceIdType.MESH
F32 = jnp.float32

ROWS, COLS, MEMB, LEV = 12, 48, 4, 128
BANDS, BLOCKS = 8, 32
SUB = 8
RUN = COLS // SUB
UNITS = MEMB * RUN
SHARE = UNITS // BANDS
NLAT = ROWS * BANDS
HALF = SHARE * SUB


def lat_partner(band, step):
    hop = step // 2
    away = (2 + hop + hop // 2 + 2 * (hop // 3)) % (BANDS // 2)
    other = (step + hop // 3) % 2
    return (band // 2 + away) % (BANDS // 2) * 2 + (band + other) % 2


def rows_at(start, count=SUB):
    return pl.ds(pl.multiple_of(start, SUB), count)


def wide(row, rows=SUB):
    return jnp.broadcast_to(row, (rows, LEV))


def parts_of(value):
    high = value.astype(jnp.bfloat16)
    return high, (value - high.astype(F32)).astype(jnp.bfloat16)


def product(left, right):
    return jnp.dot(left, right, preferred_element_type=F32)


def sublane_sums(vals):
    sub = lax.broadcasted_iota(jnp.int32, (SUB, LEV), 0)
    low = sub < 4
    four = [
        jnp.where(low, vals[k], vals[k + 4]) + pltpu.roll(jnp.where(low, vals[k + 4], vals[k]), 4, 0)
        for k in range(4)
    ]
    low = sub % 4 < 2
    two = [
        jnp.where(low, four[k] + pltpu.roll(four[k], 6, 0), four[k + 2] + pltpu.roll(four[k + 2], 2, 0))
        for k in range(2)
    ]
    low = sub % 2 < 1
    return jnp.where(low, two[0] + pltpu.roll(two[0], 7, 0), two[1] + pltpu.roll(two[1], 1, 0))


def sums_before(val):
    sub = lax.broadcasted_iota(jnp.int32, (SUB, LEV), 0)
    val = jnp.where(sub >= 1, pltpu.roll(val, 1, 0), 0.0)
    for step in (1, 2, 4):
        val = val + jnp.where(sub >= step, pltpu.roll(val, step, 0), 0.0)
    return val


def sums_after(val):
    sub = lax.broadcasted_iota(jnp.int32, (SUB, LEV), 0)
    val = jnp.where(sub < SUB - 1, pltpu.roll(val, SUB - 1, 0), 0.0)
    for step in (1, 2, 4):
        val = val + jnp.where(sub < SUB - step, pltpu.roll(val, SUB - step, 0), 0.0)
    return val


def kernel(
    e_hbm, g_hbm, norm_hbm, lon_hbm, lat_hbm, diag_hbm, below_hbm, out_v,
    e_v, g_v, norm_ref, lon_ref, lat_ref, diag_ref, below_ref, y_v,
    tmp, rk_t, phi_t, w1_t, n_t, phin_t, w1n_t,
    w1n_e, phin_e, w1_e, phi_e,
    lat_pad, lat_rk, lat_rows, lat_t, w1l_e, phil_e, cw1_e, cphi_e,
    vinv,
    cs_a, cr_a, ss_a, sr_a, ts_a, tr_a, rows_a, inv_a,
    cs_b, cr_b, ss_b, sr_b, ts_b, tr_b, rows_b, tb_b, el_b,
    load_sem,
    ca_send, ca_recv, sa_send, sa_recv, ta_send, ta_recv,
    cb_send, cb_recv, sb_send, sb_recv, tb_send, tb_recv,
):
    band = lax.axis_index("lat")
    me = lax.axis_index("lon")
    is_solver = me < ROWS
    my_row = me % ROWS

    pairs = (
        (lon_hbm, lon_ref), (norm_hbm, norm_ref), (lat_hbm, lat_ref), (g_hbm, g_v), (e_hbm, e_v),
        (diag_hbm, diag_ref), (below_hbm, below_ref),
    )
    loads = [pltpu.make_async_copy(*pair, load_sem.at[k]) for k, pair in enumerate(pairs)]
    for copy in loads:
        copy.start()

    barrier = pltpu.get_barrier_semaphore()

    def greet_lon(step, _):
        pl.semaphore_signal(barrier, inc=1, device_id=(band, (me + step) % BLOCKS), device_id_type=MESH)
        return 0

    def greet_lat(step, _):
        pl.semaphore_signal(barrier, inc=1, device_id=((band + step) % BANDS, me), device_id_type=MESH)
        return 0

    @pl.when(is_solver)
    def _():
        lax.fori_loop(1, BLOCKS, greet_lon, 0)

    lax.fori_loop(1, BANDS, greet_lat, 0)

    tmp[...] = jnp.full((LEV, LEV), 2048.0, F32)
    loads[0].wait()
    loads[1].wait()
    tmp[0:ROWS, 0:COLS] = lon_ref[...]
    rk_t[...] = 1.0 / tmp[...].T[0:COLS]
    tmp[0:ROWS, 0:COLS] = norm_ref[...]
    n_t[...] = tmp[...].T[0:COLS]
    flow_p = jnp.zeros((1, LEV), F32)
    flow_s = jnp.zeros((1, LEV), F32)
    val_p = rk_t[0:1]
    val_s = rk_t[COLS - 1 : COLS]
    phi_t[0:1] = jnp.zeros((1, LEV), F32)
    phi_t[1:2] = val_p
    w1_t[COLS - 1 : COLS] = val_s
    for i in range(1, COLS):
        flow_p = flow_p + val_p
        val_p = val_p + (1.0 + flow_p) * rk_t[i : i + 1]
        if i < COLS - 1:
            phi_t[i + 1 : i + 2] = val_p
        k = COLS - i
        flow_s = flow_s + val_s
        val_s = val_s + (1.0 + flow_s) * rk_t[k - 1 : k]
        w1_t[k - 1 : k] = val_s
    edge = 1.0 / val_p
    scale = 1.0 / val_s
    lane = lax.broadcasted_iota(jnp.int32, (SUB, LEV), 1)
    own = pltpu.roll(wide(1.0 + flow_s * scale), 16, 1)
    after = pltpu.roll(wide(flow_p * edge), 32, 1)
    cs_a[...] = jnp.where(lane < 16, wide(edge), jnp.where(lane < 32, own, after))
    w1_t[...] = w1_t[...] * scale
    w1n_t[...] = w1_t[...] * n_t[...]
    phin_t[...] = phi_t[...] * n_t[...]

    @pl.when(is_solver)
    def _():
        pl.semaphore_wait(barrier, ROWS + BANDS - 2)

    @pl.when(jnp.logical_not(is_solver))
    def _():
        pl.semaphore_wait(barrier, ROWS + BANDS - 1)

    def coeff_copy_a(row):
        return pltpu.make_async_remote_copy(
            src_ref=cs_a.at[pl.ds(0, 1)],
            dst_ref=cr_a.at[pl.ds(me, 1)],
            send_sem=ca_send.at[row],
            recv_sem=ca_recv,
            device_id=(band, row),
            device_id_type=MESH,
        )

    def rhs_copy_a(row):
        return pltpu.make_async_remote_copy(
            src_ref=ss_a.at[rows_at(row * SUB)],
            dst_ref=sr_a.at[rows_at(me * SUB)],
            send_sem=sa_send.at[row],
            recv_sem=sa_recv,
            device_id=(band, row),
            device_id_type=MESH,
        )

    def back_copy_a(target):
        return pltpu.make_async_remote_copy(
            src_ref=ts_a.at[rows_at(target * SUB)],
            dst_ref=tr_a.at[rows_at(my_row * SUB)],
            send_sem=ta_send.at[target],
            recv_sem=ta_recv.at[my_row],
            device_id=(band, target),
            device_id_type=MESH,
        )

    def copy_b(kind, target):
        size = SUB if kind == 0 else 2 * HALF
        source = (cs_b, ss_b, ts_b)[kind]
        dest = (cr_b, sr_b, tr_b)[kind]
        return pltpu.make_async_remote_copy(
            src_ref=source if kind == 0 else source.at[rows_at(target * size, size)],
            dst_ref=dest.at[rows_at(band * size, size)],
            send_sem=(cb_send, sb_send, tb_send)[kind].at[target],
            recv_sem=(cb_recv, sb_recv, tb_recv)[kind].at[band],
            device_id=(target, me),
            device_id_type=MESH,
        )

    def landed_b(kind, source):
        size = SUB if kind == 0 else 2 * HALF
        dest = (cr_b, sr_b, tr_b)[kind]
        slot = dest.at[rows_at(source * size, size)]
        return pltpu.make_async_copy(slot, slot, (cb_recv, sb_recv, tb_recv)[kind].at[source])

    def send_coeff_a(step, _):
        row = (me + step) % ROWS

        @pl.when(row != me)
        def _():
            coeff_copy_a(row).start()

        return 0

    lax.fori_loop(0, ROWS, send_coeff_a, 0)

    @pl.when(is_solver)
    def _():
        cr_a[pl.ds(me, 1)] = cs_a[0:1]

    lat_pad[...] = jnp.full((16, LEV), 512.0, F32)
    loads[2].wait()
    lat_pad[0:ROWS, 0:COLS] = lat_ref[...]
    lat_rk[...] = 1.0 / lat_pad[...]
    at = band * ROWS + lax.broadcasted_iota(jnp.int32, (16, LEV), 0)
    at = jnp.minimum(at, NLAT - 1 - at).astype(F32)
    angle = (at + 0.5) * (math.pi / NLAT)
    square = angle * angle
    series = jnp.full((16, LEV), 1.0 / math.factorial(13), F32)
    for power in (11, 9, 7, 5, 3, 1):
        series = 1.0 / math.factorial(power) - series * square
    lat_t[0:16] = angle * series

    def cosine(j):
        return lat_t[j : j + 1]

    last = jnp.where(band == BANDS - 1, 0.0, 1.0) * lat_pad[ROWS - 1 : ROWS]
    lat_rows[...] = jnp.zeros((LEV, LEV), F32)
    flow_p = jnp.zeros((1, LEV), F32)
    flow_s = jnp.zeros((1, LEV), F32)
    val_p = lat_rk[0:1]
    val_s = jnp.ones((1, LEV), F32)
    lat_rows[17:18] = val_p
    lat_rows[ROWS - 1 : ROWS] = val_s
    for j in range(1, ROWS):
        flow_p = flow_p + cosine(j) * val_p
        if j < ROWS - 1:
            val_p = val_p + (1.0 + flow_p) * lat_rk[j : j + 1]
            lat_rows[17 + j : 18 + j] = val_p
        k = ROWS - j
        flow_s = flow_s + cosine(k) * val_s
        val_s = val_s + (last + flow_s) * lat_rk[k - 1 : k]
        lat_rows[k - 1 : k] = val_s
    edge = last / (last * val_p + 1.0 + flow_p)
    scale = 1.0 / val_s
    cs_b[...] = jnp.zeros((SUB, LEV), F32)
    cs_b[0:1] = edge
    cs_b[1:2] = cosine(0) + flow_s * scale
    cs_b[2:3] = flow_p * edge
    lat_rows[0:16] = lat_rows[0:16] * scale
    lat_rows[32:48] = lat_rows[0:16] * lat_t[0:16]
    lat_rows[48:64] = lat_rows[16:32] * lat_t[0:16]

    def send_coeff_b(step, _):
        copy_b(0, (band + step) % BANDS).start()
        return 0

    lax.fori_loop(1, BANDS, send_coeff_b, 0)
    cr_b[rows_at(band * SUB)] = cs_b[...]

    for t in range(RUN):
        for source, target in ((w1n_t, w1n_e), (phin_t, phin_e)):
            part = source[pl.ds(t, SUB, stride=RUN), :]
            for j in range(ROWS):
                at = j * COLS + t * SUB
                target[at : at + SUB] = jnp.broadcast_to(part[:, j : j + 1], (SUB, LEV))

    loads[3].wait()
    loads[4].wait()

    def contribute(step, _):
        row = (me + step) % ROWS
        sums = [jnp.zeros((SUB, LEV), F32) for _ in range(2 * MEMB)]
        for t in range(RUN):
            grad = g_v[pl.ds(row * COLS + t, SUB, stride=RUN), :]
            first = w1n_e[rows_at(row * COLS + t * SUB)] * grad
            second = phin_e[rows_at(row * COLS + t * SUB)] * grad
            for m in range(MEMB):
                value = e_v[pl.ds(row * COLS * MEMB + t * MEMB + m, SUB, stride=RUN * MEMB), :]
                sums[m] = sums[m] + first * value
                sums[MEMB + m] = sums[MEMB + m] + second * value
        ss_a[rows_at(row * SUB)] = sublane_sums(sums)

        @pl.when(row != me)
        def _():
            rhs_copy_a(row).start()

        return 0

    lax.fori_loop(0, ROWS, contribute, 0)

    @pl.when(is_solver)
    def _():
        sr_a[rows_at(me * SUB)] = ss_a[rows_at(my_row * SUB)]

    loads[5].wait()
    loads[6].wait()
    tmp[0:SUB] = jnp.zeros((SUB, LEV), F32)
    tmp[0:1, 0 : LEV - 1] = below_ref[...]
    dinv = 1.0 / wide(diag_ref[...])
    lane = lax.broadcasted_iota(jnp.int32, (SUB, LEV), 1)
    ratio = jnp.where(lane == 0, 0.0, -pltpu.roll(wide(tmp[0:1]), 1, 1) * dinv)
    row_ids = lax.broadcasted_iota(jnp.int32, (LEV, LEV), 0)
    col_ids = lax.broadcasted_iota(jnp.int32, (LEV, LEV), 1)
    half = jnp.where(row_ids == col_ids, wide(dinv[0:1], LEV), 0.0)
    step = 1
    while step < LEV:
        half = half + wide(ratio[0:1], LEV) * pltpu.roll(half, step, 1)
        ratio = ratio * pltpu.roll(ratio, step, 1)
        step *= 2
    vinv[...] = lax.dot_general(
        half, half, (((1,), (1,)), ((), ())), precision=HIGHEST, preferred_element_type=F32
    )

    for t in range(RUN):
        for source, target in ((w1_t, w1_e), (phi_t, phi_e)):
            part = source[pl.ds(t, SUB, stride=RUN), :]
            for j in range(ROWS):
                at = j * COLS + t * SUB
                target[at : at + SUB] = jnp.broadcast_to(part[:, j : j + 1], (SUB, LEV))

    def interior(row, _):
        firsts, seconds = [], []
        for t in range(RUN):
            grad = g_v[pl.ds(row * COLS + t, SUB, stride=RUN), :]
            firsts.append(w1n_e[rows_at(row * COLS + t * SUB)] * grad)
            seconds.append(phin_e[rows_at(row * COLS + t * SUB)] * grad)
        for m in range(MEMB):
            values = [
                e_v[pl.ds(row * COLS * MEMB + t * MEMB + m, SUB, stride=RUN * MEMB), :] for t in range(RUN)
            ]
            ahead = [seconds[0] * values[0]]
            for t in range(1, RUN):
                ahead.append(ahead[-1] + seconds[t] * values[t])
            behind = [None] * RUN
            total = jnp.zeros((SUB, LEV), F32)
            for t in reversed(range(RUN)):
                behind[t] = total
                total = total + firsts[t] * values[t]
            before = sums_before(ahead[-1])
            after = sums_after(total)
            for t in range(RUN):
                w1 = w1_e[rows_at(row * COLS + t * SUB)]
                phi = phi_e[rows_at(row * COLS + t * SUB)]
                y_v[rows_at(((m * RUN + t) * ROWS + row) * SUB)] = w1 * (before + ahead[t]) + phi * (
                    after + behind[t]
                )
        return 0

    lax.fori_loop(0, ROWS, interior, 0)

    size = UNITS * SUB

    def vertical(part, _):
        at = rows_at(part * size, size)
        y_v[at] = jnp.dot(y_v[at], vinv[...], precision=HIGHEST, preferred_element_type=F32)
        return 0

    lax.fori_loop(0, ROWS, vertical, 0)

    lat_t[...] = lat_rows[...].T
    for t in range(RUN):
        part = lat_t[pl.ds(t, SUB, stride=RUN), :]
        for number, target in enumerate((w1l_e, phil_e, cw1_e, cphi_e)):
            for j in range(ROWS):
                at = j * COLS + t * SUB
                lane_at = number * 16 + j
                target[at : at + SUB] = jnp.broadcast_to(part[:, lane_at : lane_at + 1], (SUB, LEV))

    def wait_coeff_b(step, _):
        landed_b(0, (band + step) % BANDS).wait()
        return 0

    lax.fori_loop(1, BANDS, wait_coeff_b, 0)
    flow_p = jnp.zeros((1, LEV), F32)
    flow_s = jnp.zeros((1, LEV), F32)
    val_p = jnp.ones((1, LEV), F32)
    val_s = jnp.ones((1, LEV), F32)

    def band_base(p):
        own = cr_b[p * SUB + 1 : p * SUB + 2]
        return own if p == 0 else own + cr_b[(p - 1) * SUB + 2 : (p - 1) * SUB + 3]

    def band_link(p):
        return cr_b[p * SUB : p * SUB + 1]

    rows_b[...] = jnp.zeros((LEV, LEV), F32)
    rows_b[0:1] = val_p
    rows_b[2 * BANDS - 1 : 2 * BANDS] = val_s
    for p in range(BANDS - 1):
        flow_p = flow_p + band_base(p) * val_p
        val_p = val_p + flow_p / band_link(p)
        rows_b[p + 1 : p + 2] = val_p
        k = BANDS - 1 - p
        flow_s = flow_s + band_base(k) * val_s
        val_s = val_s + flow_s / band_link(k - 1)
        rows_b[BANDS + k - 1 : BANDS + k] = val_s
    flow_s = flow_s + band_base(0) * val_s
    rows_b[BANDS : 2 * BANDS] = rows_b[BANDS : 2 * BANDS] * (1.0 / flow_s)
    for p in range(BANDS - 1):
        rows_b[2 * BANDS + p : 2 * BANDS + p + 1] = band_link(p)
    tb_b[...] = rows_b[...].T
    for tt in range(SHARE):
        part = tb_b[pl.ds((band % 2) * SHARE + tt, SUB, stride=RUN), :]
        for number in range(3 * BANDS):
            at = (number * SHARE + tt) * SUB
            el_b[at : at + SUB] = jnp.broadcast_to(part[:, number : number + 1], (SUB, LEV))

    @pl.when(is_solver)
    def _():
        slots = cr_a.at[pl.ds(0, BLOCKS - 1)]
        pltpu.make_async_copy(slots, slots, ca_recv).wait()
        link = cr_a[...]
        base = pltpu.roll(link, LEV - 16, 1) + pltpu.roll(pltpu.roll(link, LEV - 32, 1), 1, 0)
        rows_a[0:BLOCKS] = 1.0 / link
        rows_a[BLOCKS : 2 * BLOCKS] = base
        flow_p = jnp.zeros((1, LEV), F32)
        flow_s = jnp.zeros((1, LEV), F32)
        val_p = rows_a[0:1]
        val_s = rows_a[BLOCKS - 1 : BLOCKS]
        tmp[0:1] = jnp.zeros((1, LEV), F32)
        tmp[1:2] = val_p
        tmp[2 * BLOCKS - 1 : 2 * BLOCKS] = val_s
        for p in range(1, BLOCKS):
            flow_p = flow_p + rows_a[BLOCKS + p : BLOCKS + p + 1] * val_p
            val_p = val_p + (1.0 + flow_p) * rows_a[p : p + 1]
            if p < BLOCKS - 1:
                tmp[p + 1 : p + 2] = val_p
            k = BLOCKS - p
            flow_s = flow_s + rows_a[BLOCKS + k : BLOCKS + k + 1] * val_s
            val_s = val_s + (1.0 + flow_s) * rows_a[k - 1 : k]
            tmp[BLOCKS + k - 1 : BLOCKS + k] = val_s
        first = tmp[BLOCKS : 2 * BLOCKS] * (1.0 / val_s)
        both = first + tmp[0:BLOCKS] * (1.0 / val_p)
        total = jnp.sum(both * base, axis=0, keepdims=True)
        tmp[BLOCKS : 2 * BLOCKS] = first
        tmp[2 * BLOCKS : 3 * BLOCKS] = both * (1.0 / total)
        tmp[3 * BLOCKS : 4 * BLOCKS] = both
        whole = tmp[...]
        lanes = lax.broadcasted_iota(jnp.int32, (LEV, LEV), 1)
        column = jnp.sum(jnp.where(lanes == my_row, whole, 0.0), axis=1, keepdims=True)
        column = jnp.broadcast_to(column, (LEV, LEV))
        tmp[...] = whole.T
        line = wide(tmp[pl.ds(my_row, 1), :])
        phi_row = wide(line[0:1], BLOCKS)
        first_row = wide(pltpu.roll(line, LEV - BLOCKS, 1)[0:1], BLOCKS)
        both_row = wide(pltpu.roll(line, LEV - 2 * BLOCKS, 1)[0:1], BLOCKS)
        sub_ids = lax.broadcasted_iota(jnp.int32, (BLOCKS, LEV), 0)
        lane_ids = lax.broadcasted_iota(jnp.int32, (BLOCKS, LEV), 1)
        inv_a[0:BLOCKS] = (
            jnp.where(
                sub_ids <= lane_ids,
                column[0:BLOCKS] * first_row,
                column[BLOCKS : 2 * BLOCKS] * phi_row,
            )
            + column[3 * BLOCKS : 4 * BLOCKS] * both_row
        )
        link = jnp.sum(jnp.where(lane_ids == my_row, link, 0.0), axis=1, keepdims=True)
        inv_a[BLOCKS : 2 * BLOCKS] = jnp.broadcast_to(link, (BLOCKS, LEV))

    @pl.when(is_solver)
    def _():
        slots = sr_a.at[rows_at(0, (BLOCKS - 1) * SUB)]
        pltpu.make_async_copy(slots, slots, sa_recv).wait()
        link = inv_a[BLOCKS : 2 * BLOCKS]
        inv_high, inv_low = parts_of(inv_a[0:BLOCKS][:, 0:BLOCKS])
        vinv_high, vinv_low = parts_of(vinv[...])
        rhs = []
        for m in range(MEMB):
            own = sr_a[pl.ds(m, BLOCKS, stride=SUB), :]
            after = sr_a[pl.ds(MEMB + m, BLOCKS, stride=SUB), :]
            rhs.append(own + pltpu.roll(link * after, 1, 0))
        high, low = parts_of(jnp.concatenate(rhs, axis=0))
        rhs = product(high, vinv_high) + product(high, vinv_low) + product(low, vinv_high)
        high, low = parts_of(
            jnp.concatenate([rhs[m * BLOCKS : (m + 1) * BLOCKS] for m in range(MEMB)], axis=1)
        )
        solved = product(inv_high, high) + product(inv_high, low) + product(inv_low, high)
        for m in range(MEMB):
            found = solved[:, m * LEV : (m + 1) * LEV]
            ts_a[pl.ds(m, BLOCKS, stride=SUB), :] = found
            ts_a[pl.ds(MEMB + m, BLOCKS, stride=SUB), :] = link * pltpu.roll(found, BLOCKS - 1, 0)

        def send_back(target, _):
            @pl.when(target != me)
            def _():
                back_copy_a(target).start()

            return 0

        lax.fori_loop(0, BLOCKS, send_back, 0)
        tr_a[rows_at(my_row * SUB)] = ts_a[rows_at(me * SUB)]

    def wait_back_a(row, _):
        @pl.when(row != me)
        def _():
            slot = tr_a.at[rows_at(row * SUB)]
            pltpu.make_async_copy(slot, slot, ta_recv.at[row]).wait()

        return 0

    lax.fori_loop(0, ROWS, wait_back_a, 0)

    def finish_lon(step, _):
        share = lat_partner(band, step)
        m = share // 2
        for tt in range(SHARE):
            t = (share % 2) * SHARE + tt
            own = jnp.zeros((SUB, LEV), F32)
            after = jnp.zeros((SUB, LEV), F32)
            for j in range(ROWS):
                at = rows_at(((share * SHARE + tt) * ROWS + j) * SUB)
                coeff = rows_at(j * COLS + t * SUB)
                sep_own = wide(tr_a[pl.ds(j * SUB + m, 1), :])
                sep_next = wide(tr_a[pl.ds(j * SUB + MEMB + m, 1), :])
                value = y_v[at] + w1_e[coeff] * sep_own + phi_e[coeff] * sep_next
                y_v[at] = value
                own = own + w1l_e[coeff] * value
                after = after + phil_e[coeff] * value
            ss_b[rows_at(share * 2 * HALF + tt * SUB)] = own
            ss_b[rows_at(share * 2 * HALF + HALF + tt * SUB)] = after

        @pl.when(share != band)
        def _():
            copy_b(1, share).start()

        return 0

    lax.fori_loop(0, BANDS, finish_lon, 0)
    sr_b[rows_at(band * 2 * HALF, 2 * HALF)] = ss_b[rows_at(band * 2 * HALF, 2 * HALF)]

    def interior_lat(unit, _):
        t = unit % RUN
        total = jnp.zeros((SUB, LEV), F32)
        aheads = []
        for j in range(ROWS):
            at = rows_at((unit * ROWS + j) * SUB)
            total = total + phil_e[rows_at(j * COLS + t * SUB)] * y_v[at]
            aheads.append(total)
        total = jnp.zeros((SUB, LEV), F32)
        for j in reversed(range(ROWS)):
            at = rows_at((unit * ROWS + j) * SUB)
            coeff = rows_at(j * COLS + t * SUB)
            value = y_v[at]
            y_v[at] = cw1_e[coeff] * aheads[j] + cphi_e[coeff] * total
            total = total + w1l_e[coeff] * value
        return 0

    lax.fori_loop(0, UNITS, interior_lat, 0)

    def wait_rhs_b(step, _):
        landed_b(1, (band + step) % BANDS).wait()
        return 0

    lax.fori_loop(1, BANDS, wait_rhs_b, 0)

    for tt in range(SHARE):

        def spread(number):
            at = (number * SHARE + tt) * SUB
            return el_b[at : at + SUB]

        rhs = []
        total = jnp.zeros((SUB, LEV), F32)
        aheads = []
        for p in range(BANDS):
            at = p * 2 * HALF + tt * SUB
            value = sr_b[at : at + SUB]
            if p > 0:
                before = at - HALF
                value = value + spread(2 * BANDS + p - 1) * sr_b[before : before + SUB]
            rhs.append(value)
            total = total + spread(p) * value
            aheads.append(total)
        total = jnp.zeros((SUB, LEV), F32)
        found = None
        for p in reversed(range(BANDS)):
            at = p * 2 * HALF + tt * SUB
            if p == BANDS - 1:
                ts_b[at + HALF : at + HALF + SUB] = jnp.zeros((SUB, LEV), F32)
            else:
                ts_b[at + HALF : at + HALF + SUB] = spread(2 * BANDS + p) * found
            found = spread(BANDS + p) * aheads[p] + spread(p) * total
            ts_b[at : at + SUB] = found
            total = total + spread(BANDS + p) * rhs[p]

    def send_back_b(step, _):
        copy_b(2, lat_partner(band, step)).start()
        return 0

    lax.fori_loop(0, BANDS - 1, send_back_b, 0)
    tr_b[rows_at(band * 2 * HALF, 2 * HALF)] = ts_b[rows_at(band * 2 * HALF, 2 * HALF)]

    def sent_a(row, _):
        @pl.when(row != me)
        def _():
            coeff_copy_a(row).wait_send()
            rhs_copy_a(row).wait_send()

        return 0

    lax.fori_loop(0, ROWS, sent_a, 0)

    @pl.when(is_solver)
    def _():
        def sent_back(step, _):
            back_copy_a((me + step) % BLOCKS).wait_send()
            return 0

        lax.fori_loop(1, BLOCKS, sent_back, 0)

    def sent_b(step, _):
        for kind in range(3):
            copy_b(kind, (band + step) % BANDS).wait_send()
        return 0

    lax.fori_loop(1, BANDS, sent_b, 0)

    def finish(step, _):
        share = lat_partner(band, BANDS - 1 - step)

        @pl.when(share != band)
        def _():
            landed_b(2, share).wait()

        m = share // 2
        for tt in range(SHARE):
            t = (share % 2) * SHARE + tt
            sep_own = tr_b[rows_at(share * 2 * HALF + tt * SUB)]
            sep_next = tr_b[rows_at(share * 2 * HALF + HALF + tt * SUB)]
            for j in range(ROWS):
                at = rows_at(((share * SHARE + tt) * ROWS + j) * SUB)
                coeff = rows_at(j * COLS + t * SUB)
                out_v[pl.ds(j * COLS * MEMB + t * MEMB + m, SUB, stride=RUN * MEMB), :] = (
                    y_v[at] + cw1_e[coeff] * sep_own + cphi_e[coeff] * sep_next
                )
        return 0

    lax.fori_loop(0, BANDS, finish, 0)


def shards(
    ensemble, grad_increment, normalization, lon_diffusion, lat_diffusion, vert_diag, vert_sub
):
    block = ROWS * COLS * MEMB
    anywhere = pl.BlockSpec(memory_space=pl.ANY)

    def buf(rows):
        return pltpu.VMEM((rows, LEV), F32)

    coeffs = ROWS * COLS
    dma = pltpu.SemaphoreType.DMA
    scratch = [
        buf(block), buf(coeffs), *[pltpu.VMEM((ROWS, COLS), F32)] * 3, buf(1), pltpu.VMEM((1, LEV - 1), F32),
        buf(block),
        buf(LEV), *[buf(COLS)] * 6,
        *[buf(coeffs)] * 4,
        buf(16), buf(16), buf(LEV), buf(LEV), *[buf(coeffs)] * 4,
        buf(LEV),
        buf(SUB), buf(BLOCKS), buf(ROWS * SUB), buf(BLOCKS * SUB), buf(BLOCKS * SUB), buf(ROWS * SUB),
        buf(2 * BLOCKS), buf(2 * BLOCKS),
        buf(SUB), buf(BANDS * SUB), *[buf(BANDS * 2 * HALF)] * 4,
        buf(LEV), buf(LEV), buf(3 * BANDS * HALF),
        dma((7,)),
        dma((ROWS,)), dma, dma((ROWS,)), dma, dma((BLOCKS,)), dma((ROWS,)),
        *[dma((BANDS,))] * 6,
    ]
    out = pl.pallas_call(
        kernel,
        out_shape=pltpu.VMEM((block, LEV), F32),
        in_specs=[anywhere] * 7,
        out_specs=pl.BlockSpec(memory_space=pltpu.VMEM),
        scratch_shapes=scratch,
        compiler_params=pltpu.CompilerParams(
            collective_id=0, has_side_effects=True, vmem_limit_bytes=60 * 1024 * 1024
        ),
    )(
        ensemble.reshape(block, LEV),
        grad_increment.reshape(coeffs, LEV),
        normalization,
        lon_diffusion,
        lat_diffusion,
        vert_diag.reshape(1, LEV),
        vert_sub.reshape(1, LEV - 1),
    )
    return out.reshape(ROWS, COLS, MEMB, LEV)


def solution(mesh):
    in_specs = (
        P("lat", "lon", None, None),
        P("lat", "lon", None),
        P("lat", "lon"),
        P("lat", "lon"),
        P("lat", "lon"),
        P(),
        P(),
    )
    out_specs = P("lat", "lon", None, None)
    return jax.shard_map(shards, mesh=mesh, in_specs=in_specs, out_specs=out_specs, check_vma=False)
```

```python
import functools
import math

import jax
import jax.numpy as jnp
from jax import lax
from jax.experimental import pallas as pl
from jax.experimental.pallas import tpu as pltpu
from jax.sharding import PartitionSpec as P

HIGHEST = lax.Precision.HIGHEST
MESH = pl.DeviceIdType.MESH
F32 = jnp.float32

ROWS, COLS, MEMB, LEV = 12, 48, 4, 128
BANDS, BLOCKS = 8, 32
SUB = 8
RUN = COLS // SUB
UNITS = MEMB * RUN
SHARE = UNITS // BANDS
NLAT = ROWS * BANDS
HALF = SHARE * SUB
SOLVERS = 6
GROUP = ROWS // SOLVERS
PACK = GROUP * SUB
FIRST = 4


def lat_partner(band, step):
    hop = step // 2
    away = (2 + hop + hop // 2 + 2 * (hop // 3)) % (BANDS // 2)
    other = (step + hop // 3) % 2
    return (band // 2 + away) % (BANDS // 2) * 2 + (band + other) % 2


def rows_at(start, count=SUB):
    return pl.ds(pl.multiple_of(start, SUB), count)


def wide(row, rows=SUB):
    return jnp.broadcast_to(row, (rows, LEV))


def parts_of(value):
    high = value.astype(jnp.bfloat16)
    return high, (value - high.astype(F32)).astype(jnp.bfloat16)


def product(left, right):
    return jnp.dot(left, right, preferred_element_type=F32)


def sublane_sums(vals):
    sub = lax.broadcasted_iota(jnp.int32, (SUB, LEV), 0)
    low = sub < 4
    four = [
        jnp.where(low, vals[k], vals[k + 4]) + pltpu.roll(jnp.where(low, vals[k + 4], vals[k]), 4, 0)
        for k in range(4)
    ]
    low = sub % 4 < 2
    two = [
        jnp.where(low, four[k] + pltpu.roll(four[k], 6, 0), four[k + 2] + pltpu.roll(four[k + 2], 2, 0))
        for k in range(2)
    ]
    low = sub % 2 < 1
    return jnp.where(low, two[0] + pltpu.roll(two[0], 7, 0), two[1] + pltpu.roll(two[1], 1, 0))


def sums_before(val):
    sub = lax.broadcasted_iota(jnp.int32, (SUB, LEV), 0)
    val = jnp.where(sub >= 1, pltpu.roll(val, 1, 0), 0.0)
    for step in (1, 2, 4):
        val = val + jnp.where(sub >= step, pltpu.roll(val, step, 0), 0.0)
    return val


def sums_after(val):
    sub = lax.broadcasted_iota(jnp.int32, (SUB, LEV), 0)
    val = jnp.where(sub < SUB - 1, pltpu.roll(val, SUB - 1, 0), 0.0)
    for step in (1, 2, 4):
        val = val + jnp.where(sub < SUB - step, pltpu.roll(val, SUB - step, 0), 0.0)
    return val


def kernel(
    e_hbm, g_hbm, norm_hbm, lon_hbm, lat_hbm, diag_hbm, below_hbm, out_v,
    e_v, g_v, norm_ref, lon_ref, lat_ref, diag_ref, below_ref, y_v,
    tmp, rk_t, phi_t, w1_t, n_t, phin_t, w1n_t,
    w1n_e, phin_e, w1_e, phi_e,
    lat_pad, lat_rk, lat_rows, lat_t, w1l_e, phil_e, cw1_e, cphi_e,
    vinv,
    cs_a, cr_a, ss_a, sr_a, ts_a, tr_a, rows_a, inv_a,
    cs_b, cr_b, ss_b, sr_b, ts_b, tr_b, rows_b, tb_b, el_b,
    load_sem,
    ca_send, ca_recv, sa_send, sa_recv, ta_send, ta_recv,
    cb_send, cb_recv, sb_send, sb_recv, tb_send, tb_recv,
):
    band = lax.axis_index("lat")
    me = lax.axis_index("lon")
    is_solver = jnp.logical_and(me >= FIRST, me < FIRST + SOLVERS)
    place = (me + SOLVERS - FIRST) % SOLVERS
    seat = (me + BLOCKS - FIRST) % BLOCKS

    barrier = pltpu.get_barrier_semaphore()

    def greet_lon(step, _):
        away = BLOCKS // 2 + (step + 1) // 2 * (1 - step % 2 * 2)
        pl.semaphore_signal(barrier, inc=1, device_id=(band, (me + away) % BLOCKS), device_id_type=MESH)
        return 0

    def greet_lat(step, _):
        pl.semaphore_signal(barrier, inc=1, device_id=((band + step) % BANDS, me), device_id_type=MESH)
        return 0

    @pl.when(is_solver)
    def _():
        lax.fori_loop(0, BLOCKS - 1, greet_lon, 0)

    pairs = (
        (lon_hbm, lon_ref), (norm_hbm, norm_ref), (lat_hbm, lat_ref), (g_hbm, g_v), (e_hbm, e_v),
        (diag_hbm, diag_ref), (below_hbm, below_ref),
    )
    loads = [pltpu.make_async_copy(*pair, load_sem.at[k]) for k, pair in enumerate(pairs)]
    for copy in loads:
        copy.start()

    lax.fori_loop(1, BANDS, greet_lat, 0)

    tmp[...] = jnp.full((LEV, LEV), 2048.0, F32)
    loads[0].wait()
    loads[1].wait()
    tmp[0:ROWS, 0:COLS] = lon_ref[...]
    rk_t[...] = 1.0 / tmp[...].T[0:COLS]
    tmp[0:ROWS, 0:COLS] = norm_ref[...]
    n_t[...] = tmp[...].T[0:COLS]
    flow_p = jnp.zeros((1, LEV), F32)
    flow_s = jnp.zeros((1, LEV), F32)
    val_p = rk_t[0:1]
    val_s = rk_t[COLS - 1 : COLS]
    phi_t[0:1] = jnp.zeros((1, LEV), F32)
    phi_t[1:2] = val_p
    w1_t[COLS - 1 : COLS] = val_s
    for i in range(1, COLS):
        flow_p = flow_p + val_p
        val_p = val_p + (1.0 + flow_p) * rk_t[i : i + 1]
        if i < COLS - 1:
            phi_t[i + 1 : i + 2] = val_p
        k = COLS - i
        flow_s = flow_s + val_s
        val_s = val_s + (1.0 + flow_s) * rk_t[k - 1 : k]
        w1_t[k - 1 : k] = val_s
    edge = 1.0 / val_p
    scale = 1.0 / val_s
    lane = lax.broadcasted_iota(jnp.int32, (SUB, LEV), 1)
    own = pltpu.roll(wide(1.0 + flow_s * scale), 16, 1)
    after = pltpu.roll(wide(flow_p * edge), 32, 1)
    cs_a[...] = jnp.where(lane < 16, wide(edge), jnp.where(lane < 32, own, after))
    w1_t[...] = w1_t[...] * scale
    w1n_t[...] = w1_t[...] * n_t[...]
    phin_t[...] = phi_t[...] * n_t[...]

    @pl.when(is_solver)
    def _():
        pl.semaphore_wait(barrier, SOLVERS + BANDS - 2)

    @pl.when(jnp.logical_not(is_solver))
    def _():
        pl.semaphore_wait(barrier, SOLVERS + BANDS - 1)

    def coeff_copy_a(solver):
        return pltpu.make_async_remote_copy(
            src_ref=cs_a.at[pl.ds(0, 1)],
            dst_ref=cr_a.at[pl.ds(me, 1)],
            send_sem=ca_send.at[solver],
            recv_sem=ca_recv,
            device_id=(band, solver + FIRST),
            device_id_type=MESH,
        )

    def rhs_copy_a(solver):
        return pltpu.make_async_remote_copy(
            src_ref=ss_a.at[rows_at(solver * PACK, PACK)],
            dst_ref=sr_a.at[rows_at(me * PACK, PACK)],
            send_sem=sa_send.at[solver],
            recv_sem=sa_recv,
            device_id=(band, solver + FIRST),
            device_id_type=MESH,
        )

    def back_copy_a(target):
        return pltpu.make_async_remote_copy(
            src_ref=ts_a.at[rows_at(target * PACK, PACK)],
            dst_ref=tr_a.at[rows_at(place * PACK, PACK)],
            send_sem=ta_send.at[target],
            recv_sem=ta_recv.at[place],
            device_id=(band, target),
            device_id_type=MESH,
        )

    def copy_b(kind, target):
        size = SUB if kind == 0 else 2 * HALF
        source = (cs_b, ss_b, ts_b)[kind]
        dest = (cr_b, sr_b, tr_b)[kind]
        return pltpu.make_async_remote_copy(
            src_ref=source if kind == 0 else source.at[rows_at(target * size, size)],
            dst_ref=dest.at[rows_at(band * size, size)],
            send_sem=(cb_send, sb_send, tb_send)[kind].at[target],
            recv_sem=(cb_recv, sb_recv, tb_recv)[kind].at[band],
            device_id=(target, me),
            device_id_type=MESH,
        )

    def landed_b(kind, source):
        size = SUB if kind == 0 else 2 * HALF
        dest = (cr_b, sr_b, tr_b)[kind]
        slot = dest.at[rows_at(source * size, size)]
        return pltpu.make_async_copy(slot, slot, (cb_recv, sb_recv, tb_recv)[kind].at[source])

    def send_coeff_a(step, _):
        solver = (me + step) % SOLVERS

        @pl.when(solver != seat)
        def _():
            coeff_copy_a(solver).start()

        return 0

    lax.fori_loop(0, SOLVERS, send_coeff_a, 0)

    @pl.when(is_solver)
    def _():
        cr_a[pl.ds(me, 1)] = cs_a[0:1]

    for t in range(RUN):
        for source, target in ((w1n_t, w1n_e), (phin_t, phin_e)):
            part = source[pl.ds(t, SUB, stride=RUN), :]
            for j in range(ROWS):
                at = j * COLS + t * SUB
                target[at : at + SUB] = jnp.broadcast_to(part[:, j : j + 1], (SUB, LEV))

    loads[3].wait()
    loads[4].wait()

    def contribute(step, _):
        solver = (me + step) % SOLVERS
        for g in range(GROUP):
            row = solver * GROUP + g
            sums = [jnp.zeros((SUB, LEV), F32) for _ in range(2 * MEMB)]
            for t in range(RUN):
                grad = g_v[pl.ds(row * COLS + t, SUB, stride=RUN), :]
                first = w1n_e[rows_at(row * COLS + t * SUB)] * grad
                second = phin_e[rows_at(row * COLS + t * SUB)] * grad
                for m in range(MEMB):
                    value = e_v[pl.ds(row * COLS * MEMB + t * MEMB + m, SUB, stride=RUN * MEMB), :]
                    sums[m] = sums[m] + first * value
                    sums[MEMB + m] = sums[MEMB + m] + second * value
            ss_a[rows_at(row * SUB)] = sublane_sums(sums)

        @pl.when(solver != seat)
        def _():
            rhs_copy_a(solver).start()

        return 0

    lax.fori_loop(0, SOLVERS, contribute, 0)

    @pl.when(is_solver)
    def _():
        sr_a[rows_at(me * PACK, PACK)] = ss_a[rows_at(place * PACK, PACK)]

    lat_pad[...] = jnp.full((16, LEV), 512.0, F32)
    loads[2].wait()
    lat_pad[0:ROWS, 0:COLS] = lat_ref[...]
    lat_rk[...] = 1.0 / lat_pad[...]
    at = band * ROWS + lax.broadcasted_iota(jnp.int32, (16, LEV), 0)
    at = jnp.minimum(at, NLAT - 1 - at).astype(F32)
    angle = (at + 0.5) * (math.pi / NLAT)
    square = angle * angle
    series = jnp.full((16, LEV), 1.0 / math.factorial(13), F32)
    for power in (11, 9, 7, 5, 3, 1):
        series = 1.0 / math.factorial(power) - series * square
    lat_t[0:16] = angle * series

    def cosine(j):
        return lat_t[j : j + 1]

    last = jnp.where(band == BANDS - 1, 0.0, 1.0) * lat_pad[ROWS - 1 : ROWS]
    lat_rows[...] = jnp.zeros((LEV, LEV), F32)
    flow_p = jnp.zeros((1, LEV), F32)
    flow_s = jnp.zeros((1, LEV), F32)
    val_p = lat_rk[0:1]
    val_s = jnp.ones((1, LEV), F32)
    lat_rows[17:18] = val_p
    lat_rows[ROWS - 1 : ROWS] = val_s
    for j in range(1, ROWS):
        flow_p = flow_p + cosine(j) * val_p
        if j < ROWS - 1:
            val_p = val_p + (1.0 + flow_p) * lat_rk[j : j + 1]
            lat_rows[17 + j : 18 + j] = val_p
        k = ROWS - j
        flow_s = flow_s + cosine(k) * val_s
        val_s = val_s + (last + flow_s) * lat_rk[k - 1 : k]
        lat_rows[k - 1 : k] = val_s
    edge = last / (last * val_p + 1.0 + flow_p)
    scale = 1.0 / val_s
    cs_b[...] = jnp.zeros((SUB, LEV), F32)
    cs_b[0:1] = edge
    cs_b[1:2] = cosine(0) + flow_s * scale
    cs_b[2:3] = flow_p * edge
    lat_rows[0:16] = lat_rows[0:16] * scale
    lat_rows[32:48] = lat_rows[0:16] * lat_t[0:16]
    lat_rows[48:64] = lat_rows[16:32] * lat_t[0:16]

    def send_coeff_b(step, _):
        copy_b(0, (band + step) % BANDS).start()
        return 0

    lax.fori_loop(1, BANDS, send_coeff_b, 0)
    cr_b[rows_at(band * SUB)] = cs_b[...]

    loads[5].wait()
    loads[6].wait()
    tmp[0:SUB] = jnp.zeros((SUB, LEV), F32)
    tmp[0:1, 0 : LEV - 1] = below_ref[...]
    dinv = 1.0 / wide(diag_ref[...])
    lane = lax.broadcasted_iota(jnp.int32, (SUB, LEV), 1)
    ratio = jnp.where(lane == 0, 0.0, -pltpu.roll(wide(tmp[0:1]), 1, 1) * dinv)
    row_ids = lax.broadcasted_iota(jnp.int32, (LEV, LEV), 0)
    col_ids = lax.broadcasted_iota(jnp.int32, (LEV, LEV), 1)
    half = jnp.where(row_ids == col_ids, wide(dinv[0:1], LEV), 0.0)
    step = 1
    while step < LEV:
        half = half + wide(ratio[0:1], LEV) * pltpu.roll(half, step, 1)
        ratio = ratio * pltpu.roll(ratio, step, 1)
        step *= 2
    vinv[...] = lax.dot_general(
        half, half, (((1,), (1,)), ((), ())), precision=HIGHEST, preferred_element_type=F32
    )

    for t in range(RUN):
        for source, target in ((w1_t, w1_e), (phi_t, phi_e)):
            part = source[pl.ds(t, SUB, stride=RUN), :]
            for j in range(ROWS):
                at = j * COLS + t * SUB
                target[at : at + SUB] = jnp.broadcast_to(part[:, j : j + 1], (SUB, LEV))

    def interior(row, _):
        firsts, seconds = [], []
        for t in range(RUN):
            grad = g_v[pl.ds(row * COLS + t, SUB, stride=RUN), :]
            firsts.append(w1n_e[rows_at(row * COLS + t * SUB)] * grad)
            seconds.append(phin_e[rows_at(row * COLS + t * SUB)] * grad)
        for m in range(MEMB):
            values = [
                e_v[pl.ds(row * COLS * MEMB + t * MEMB + m, SUB, stride=RUN * MEMB), :] for t in range(RUN)
            ]
            ahead = [seconds[0] * values[0]]
            for t in range(1, RUN):
                ahead.append(ahead[-1] + seconds[t] * values[t])
            behind = [None] * RUN
            total = jnp.zeros((SUB, LEV), F32)
            for t in reversed(range(RUN)):
                behind[t] = total
                total = total + firsts[t] * values[t]
            before = sums_before(ahead[-1])
            after = sums_after(total)
            for t in range(RUN):
                w1 = w1_e[rows_at(row * COLS + t * SUB)]
                phi = phi_e[rows_at(row * COLS + t * SUB)]
                y_v[rows_at(((m * RUN + t) * ROWS + row) * SUB)] = w1 * (before + ahead[t]) + phi * (
                    after + behind[t]
                )
        return 0

    lax.fori_loop(0, ROWS, interior, 0)

    size = UNITS * SUB

    def vertical(part, _):
        at = rows_at(part * size, size)
        y_v[at] = jnp.dot(y_v[at], vinv[...], precision=HIGHEST, preferred_element_type=F32)
        return 0

    lax.fori_loop(0, ROWS, vertical, 0)

    lat_t[...] = lat_rows[...].T
    for t in range(RUN):
        part = lat_t[pl.ds(t, SUB, stride=RUN), :]
        for number, target in enumerate((w1l_e, phil_e, cw1_e, cphi_e)):
            for j in range(ROWS):
                at = j * COLS + t * SUB
                lane_at = number * 16 + j
                target[at : at + SUB] = jnp.broadcast_to(part[:, lane_at : lane_at + 1], (SUB, LEV))

    def wait_coeff_b(step, _):
        landed_b(0, (band + step) % BANDS).wait()
        return 0

    lax.fori_loop(1, BANDS, wait_coeff_b, 0)
    flow_p = jnp.zeros((1, LEV), F32)
    flow_s = jnp.zeros((1, LEV), F32)
    val_p = jnp.ones((1, LEV), F32)
    val_s = jnp.ones((1, LEV), F32)

    def band_base(p):
        own = cr_b[p * SUB + 1 : p * SUB + 2]
        return own if p == 0 else own + cr_b[(p - 1) * SUB + 2 : (p - 1) * SUB + 3]

    def band_link(p):
        return cr_b[p * SUB : p * SUB + 1]

    rows_b[...] = jnp.zeros((LEV, LEV), F32)
    rows_b[0:1] = val_p
    rows_b[2 * BANDS - 1 : 2 * BANDS] = val_s
    for p in range(BANDS - 1):
        flow_p = flow_p + band_base(p) * val_p
        val_p = val_p + flow_p / band_link(p)
        rows_b[p + 1 : p + 2] = val_p
        k = BANDS - 1 - p
        flow_s = flow_s + band_base(k) * val_s
        val_s = val_s + flow_s / band_link(k - 1)
        rows_b[BANDS + k - 1 : BANDS + k] = val_s
    flow_s = flow_s + band_base(0) * val_s
    rows_b[BANDS : 2 * BANDS] = rows_b[BANDS : 2 * BANDS] * (1.0 / flow_s)
    for p in range(BANDS - 1):
        rows_b[2 * BANDS + p : 2 * BANDS + p + 1] = band_link(p)
    tb_b[...] = rows_b[...].T
    for tt in range(SHARE):
        part = tb_b[pl.ds((band % 2) * SHARE + tt, SUB, stride=RUN), :]
        for number in range(3 * BANDS):
            at = (number * SHARE + tt) * SUB
            el_b[at : at + SUB] = jnp.broadcast_to(part[:, number : number + 1], (SUB, LEV))

    @pl.when(is_solver)
    def _():
        slots = cr_a.at[pl.ds(0, BLOCKS - 1)]
        pltpu.make_async_copy(slots, slots, ca_recv).wait()
        link = cr_a[...]
        base = pltpu.roll(link, LEV - 16, 1) + pltpu.roll(pltpu.roll(link, LEV - 32, 1), 1, 0)
        rows_a[0:BLOCKS] = 1.0 / link
        rows_a[BLOCKS : 2 * BLOCKS] = base
        flow_p = jnp.zeros((1, LEV), F32)
        flow_s = jnp.zeros((1, LEV), F32)
        val_p = rows_a[0:1]
        val_s = rows_a[BLOCKS - 1 : BLOCKS]
        tmp[0:1] = jnp.zeros((1, LEV), F32)
        tmp[1:2] = val_p
        tmp[2 * BLOCKS - 1 : 2 * BLOCKS] = val_s
        for p in range(1, BLOCKS):
            flow_p = flow_p + rows_a[BLOCKS + p : BLOCKS + p + 1] * val_p
            val_p = val_p + (1.0 + flow_p) * rows_a[p : p + 1]
            if p < BLOCKS - 1:
                tmp[p + 1 : p + 2] = val_p
            k = BLOCKS - p
            flow_s = flow_s + rows_a[BLOCKS + k : BLOCKS + k + 1] * val_s
            val_s = val_s + (1.0 + flow_s) * rows_a[k - 1 : k]
            tmp[BLOCKS + k - 1 : BLOCKS + k] = val_s
        first = tmp[BLOCKS : 2 * BLOCKS] * (1.0 / val_s)
        both = first + tmp[0:BLOCKS] * (1.0 / val_p)
        total = jnp.sum(both * base, axis=0, keepdims=True)
        tmp[BLOCKS : 2 * BLOCKS] = first
        tmp[2 * BLOCKS : 3 * BLOCKS] = both * (1.0 / total)
        tmp[3 * BLOCKS : 4 * BLOCKS] = both
        whole = tmp[...]
        lanes = lax.broadcasted_iota(jnp.int32, (LEV, LEV), 1)
        columns = []
        for g in range(GROUP):
            column = jnp.sum(jnp.where(lanes == place * GROUP + g, whole, 0.0), axis=1, keepdims=True)
            columns.append(jnp.broadcast_to(column, (LEV, LEV)))
        tmp[...] = whole.T
        sub_ids = lax.broadcasted_iota(jnp.int32, (BLOCKS, LEV), 0)
        lane_ids = lax.broadcasted_iota(jnp.int32, (BLOCKS, LEV), 1)
        for g, column in enumerate(columns):
            line = wide(tmp[pl.ds(place * GROUP + g, 1), :])
            phi_row = wide(line[0:1], BLOCKS)
            first_row = wide(pltpu.roll(line, LEV - BLOCKS, 1)[0:1], BLOCKS)
            both_row = wide(pltpu.roll(line, LEV - 2 * BLOCKS, 1)[0:1], BLOCKS)
            at = 2 * g * BLOCKS
            inv_a[at : at + BLOCKS] = (
                jnp.where(
                    sub_ids <= lane_ids,
                    column[0:BLOCKS] * first_row,
                    column[BLOCKS : 2 * BLOCKS] * phi_row,
                )
                + column[3 * BLOCKS : 4 * BLOCKS] * both_row
            )
            edge = jnp.sum(jnp.where(lane_ids == place * GROUP + g, link, 0.0), axis=1, keepdims=True)
            inv_a[at + BLOCKS : at + 2 * BLOCKS] = jnp.broadcast_to(edge, (BLOCKS, LEV))

    @pl.when(is_solver)
    def _():
        vinv_high, vinv_low = parts_of(vinv[...])
        slots = sr_a.at[rows_at(0, (BLOCKS - 1) * PACK)]
        pltpu.make_async_copy(slots, slots, sa_recv).wait()
        for g in range(GROUP):
            inverse = inv_a[2 * g * BLOCKS : (2 * g + 1) * BLOCKS]
            link = inv_a[(2 * g + 1) * BLOCKS : (2 * g + 2) * BLOCKS]
            inv_high, inv_low = parts_of(inverse[:, 0:BLOCKS])
            rhs = []
            for m in range(MEMB):
                own = sr_a[pl.ds(g * SUB + m, BLOCKS, stride=PACK), :]
                after = sr_a[pl.ds(g * SUB + MEMB + m, BLOCKS, stride=PACK), :]
                rhs.append(own + pltpu.roll(link * after, 1, 0))
            high, low = parts_of(jnp.concatenate(rhs, axis=0))
            rhs = product(high, vinv_high) + product(high, vinv_low) + product(low, vinv_high)
            high, low = parts_of(
                jnp.concatenate([rhs[m * BLOCKS : (m + 1) * BLOCKS] for m in range(MEMB)], axis=1)
            )
            solved = product(inv_high, high) + product(inv_high, low) + product(inv_low, high)
            for m in range(MEMB):
                found = solved[:, m * LEV : (m + 1) * LEV]
                ts_a[pl.ds(g * SUB + m, BLOCKS, stride=PACK), :] = found
                ts_a[pl.ds(g * SUB + MEMB + m, BLOCKS, stride=PACK), :] = link * pltpu.roll(found, BLOCKS - 1, 0)

        def send_back(target, _):
            @pl.when(target != me)
            def _():
                back_copy_a(target).start()

            return 0

        lax.fori_loop(0, BLOCKS, send_back, 0)
        tr_a[rows_at(place * PACK, PACK)] = ts_a[rows_at(me * PACK, PACK)]

    def wait_back_a(solver, _):
        @pl.when(solver != seat)
        def _():
            slot = tr_a.at[rows_at(solver * PACK, PACK)]
            pltpu.make_async_copy(slot, slot, ta_recv.at[solver]).wait()

        return 0

    lax.fori_loop(0, SOLVERS, wait_back_a, 0)

    def finish_lon(step, _):
        share = lat_partner(band, step)
        m = share // 2
        for tt in range(SHARE):
            t = (share % 2) * SHARE + tt
            own = jnp.zeros((SUB, LEV), F32)
            after = jnp.zeros((SUB, LEV), F32)
            for j in range(ROWS):
                at = rows_at(((share * SHARE + tt) * ROWS + j) * SUB)
                coeff = rows_at(j * COLS + t * SUB)
                sep_own = wide(tr_a[pl.ds(j * SUB + m, 1), :])
                sep_next = wide(tr_a[pl.ds(j * SUB + MEMB + m, 1), :])
                value = y_v[at] + w1_e[coeff] * sep_own + phi_e[coeff] * sep_next
                y_v[at] = value
                own = own + w1l_e[coeff] * value
                after = after + phil_e[coeff] * value
            ss_b[rows_at(share * 2 * HALF + tt * SUB)] = own
            ss_b[rows_at(share * 2 * HALF + HALF + tt * SUB)] = after

        @pl.when(share != band)
        def _():
            copy_b(1, share).start()

        return 0

    lax.fori_loop(0, BANDS, finish_lon, 0)
    sr_b[rows_at(band * 2 * HALF, 2 * HALF)] = ss_b[rows_at(band * 2 * HALF, 2 * HALF)]

    def interior_lat(unit, _):
        t = unit % RUN
        total = jnp.zeros((SUB, LEV), F32)
        aheads = []
        for j in range(ROWS):
            at = rows_at((unit * ROWS + j) * SUB)
            total = total + phil_e[rows_at(j * COLS + t * SUB)] * y_v[at]
            aheads.append(total)
        total = jnp.zeros((SUB, LEV), F32)
        for j in reversed(range(ROWS)):
            at = rows_at((unit * ROWS + j) * SUB)
            coeff = rows_at(j * COLS + t * SUB)
            value = y_v[at]
            y_v[at] = cw1_e[coeff] * aheads[j] + cphi_e[coeff] * total
            total = total + w1l_e[coeff] * value
        return 0

    lax.fori_loop(0, UNITS, interior_lat, 0)

    def wait_rhs_b(step, _):
        landed_b(1, (band + step) % BANDS).wait()
        return 0

    lax.fori_loop(1, BANDS, wait_rhs_b, 0)

    for tt in range(SHARE):

        def spread(number):
            at = (number * SHARE + tt) * SUB
            return el_b[at : at + SUB]

        rhs = []
        total = jnp.zeros((SUB, LEV), F32)
        aheads = []
        for p in range(BANDS):
            at = p * 2 * HALF + tt * SUB
            value = sr_b[at : at + SUB]
            if p > 0:
                before = at - HALF
                value = value + spread(2 * BANDS + p - 1) * sr_b[before : before + SUB]
            rhs.append(value)
            total = total + spread(p) * value
            aheads.append(total)
        total = jnp.zeros((SUB, LEV), F32)
        found = None
        for p in reversed(range(BANDS)):
            at = p * 2 * HALF + tt * SUB
            if p == BANDS - 1:
                ts_b[at + HALF : at + HALF + SUB] = jnp.zeros((SUB, LEV), F32)
            else:
                ts_b[at + HALF : at + HALF + SUB] = spread(2 * BANDS + p) * found
            found = spread(BANDS + p) * aheads[p] + spread(p) * total
            ts_b[at : at + SUB] = found
            total = total + spread(BANDS + p) * rhs[p]

    def send_back_b(step, _):
        target = (2 * step + 1 - step // (BANDS // 2)) % BANDS

        @pl.when(target != band)
        def _():
            copy_b(2, target).start()

        return 0

    lax.fori_loop(0, BANDS, send_back_b, 0)
    tr_b[rows_at(band * 2 * HALF, 2 * HALF)] = ts_b[rows_at(band * 2 * HALF, 2 * HALF)]

    def sent_a(solver, _):
        @pl.when(solver != seat)
        def _():
            coeff_copy_a(solver).wait_send()
            rhs_copy_a(solver).wait_send()

        return 0

    lax.fori_loop(0, SOLVERS, sent_a, 0)

    @pl.when(is_solver)
    def _():
        def sent_back(step, _):
            back_copy_a((me + step) % BLOCKS).wait_send()
            return 0

        lax.fori_loop(1, BLOCKS, sent_back, 0)

    def sent_b(step, _):
        for kind in range(3):
            copy_b(kind, (band + step) % BANDS).wait_send()
        return 0

    lax.fori_loop(1, BANDS, sent_b, 0)

    def finish(step, _):
        share = lat_partner(band, BANDS - 1 - step)

        @pl.when(share != band)
        def _():
            landed_b(2, share).wait()

        m = share // 2
        for tt in range(SHARE):
            t = (share % 2) * SHARE + tt
            sep_own = tr_b[rows_at(share * 2 * HALF + tt * SUB)]
            sep_next = tr_b[rows_at(share * 2 * HALF + HALF + tt * SUB)]
            for j in range(ROWS):
                at = rows_at(((share * SHARE + tt) * ROWS + j) * SUB)
                coeff = rows_at(j * COLS + t * SUB)
                out_v[pl.ds(j * COLS * MEMB + t * MEMB + m, SUB, stride=RUN * MEMB), :] = (
                    y_v[at] + cw1_e[coeff] * sep_own + cphi_e[coeff] * sep_next
                )
        return 0

    lax.fori_loop(0, BANDS, finish, 0)


def shards(
    ensemble, grad_increment, normalization, lon_diffusion, lat_diffusion, vert_diag, vert_sub
):
    block = ROWS * COLS * MEMB
    anywhere = pl.BlockSpec(memory_space=pl.ANY)

    def buf(rows):
        return pltpu.VMEM((rows, LEV), F32)

    coeffs = ROWS * COLS
    dma = pltpu.SemaphoreType.DMA
    scratch = [
        buf(block), buf(coeffs), *[pltpu.VMEM((ROWS, COLS), F32)] * 3, buf(1), pltpu.VMEM((1, LEV - 1), F32),
        buf(block),
        buf(LEV), *[buf(COLS)] * 6,
        *[buf(coeffs)] * 4,
        buf(16), buf(16), buf(LEV), buf(LEV), *[buf(coeffs)] * 4,
        buf(LEV),
        buf(SUB), buf(BLOCKS), buf(ROWS * SUB), buf(BLOCKS * PACK), buf(BLOCKS * PACK), buf(ROWS * SUB),
        buf(2 * BLOCKS), buf(2 * GROUP * BLOCKS),
        buf(SUB), buf(BANDS * SUB), *[buf(BANDS * 2 * HALF)] * 4,
        buf(LEV), buf(LEV), buf(3 * BANDS * HALF),
        dma((7,)),
        dma((SOLVERS,)), dma, dma((SOLVERS,)), dma, dma((BLOCKS,)), dma((SOLVERS,)),
        *[dma((BANDS,))] * 6,
    ]
    out = pl.pallas_call(
        kernel,
        out_shape=pltpu.VMEM((block, LEV), F32),
        in_specs=[anywhere] * 7,
        out_specs=pl.BlockSpec(memory_space=pltpu.VMEM),
        scratch_shapes=scratch,
        compiler_params=pltpu.CompilerParams(
            collective_id=0, has_side_effects=True, vmem_limit_bytes=60 * 1024 * 1024
        ),
    )(
        ensemble.reshape(block, LEV),
        grad_increment.reshape(coeffs, LEV),
        normalization,
        lon_diffusion,
        lat_diffusion,
        vert_diag.reshape(1, LEV),
        vert_sub.reshape(1, LEV - 1),
    )
    return out.reshape(ROWS, COLS, MEMB, LEV)


def solution(mesh):
    in_specs = (
        P("lat", "lon", None, None),
        P("lat", "lon", None),
        P("lat", "lon"),
        P("lat", "lon"),
        P("lat", "lon"),
        P(),
        P(),
    )
    out_specs = P("lat", "lon", None, None)
    return jax.shard_map(shards, mesh=mesh, in_specs=in_specs, out_specs=out_specs, check_vma=False)
```

```python
import functools
import math

import jax
import jax.numpy as jnp
from jax import lax
from jax.experimental import pallas as pl
from jax.experimental.pallas import tpu as pltpu
from jax.sharding import PartitionSpec as P

HIGHEST = lax.Precision.HIGHEST
MESH = pl.DeviceIdType.MESH
F32 = jnp.float32

ROWS, COLS, MEMB, LEV = 12, 48, 4, 128
BANDS, BLOCKS = 8, 32
SUB = 8
RUN = COLS // SUB
UNITS = MEMB * RUN
SHARE = UNITS // BANDS
NLAT = ROWS * BANDS
HALF = SHARE * SUB
SOLVERS = 6
GROUP = ROWS // SOLVERS
PACK = GROUP * SUB
FIRST = 4


def lat_partner(band, step):
    hop = step // 2
    away = (2 + hop + hop // 2 + 2 * (hop // 3)) % (BANDS // 2)
    other = (step + hop // 3) % 2
    return (band // 2 + away) % (BANDS // 2) * 2 + (band + other) % 2


def rows_at(start, count=SUB):
    return pl.ds(pl.multiple_of(start, SUB), count)


def wide(row, rows=SUB):
    return jnp.broadcast_to(row, (rows, LEV))


def parts_of(value):
    high = value.astype(jnp.bfloat16)
    return high, (value - high.astype(F32)).astype(jnp.bfloat16)


def product(left, right):
    return jnp.dot(left, right, preferred_element_type=F32)


def sublane_sums(vals):
    sub = lax.broadcasted_iota(jnp.int32, (SUB, LEV), 0)
    low = sub < 4
    four = [
        jnp.where(low, vals[k], vals[k + 4]) + pltpu.roll(jnp.where(low, vals[k + 4], vals[k]), 4, 0)
        for k in range(4)
    ]
    low = sub % 4 < 2
    two = [
        jnp.where(low, four[k] + pltpu.roll(four[k], 6, 0), four[k + 2] + pltpu.roll(four[k + 2], 2, 0))
        for k in range(2)
    ]
    low = sub % 2 < 1
    return jnp.where(low, two[0] + pltpu.roll(two[0], 7, 0), two[1] + pltpu.roll(two[1], 1, 0))


def sums_before(val):
    sub = lax.broadcasted_iota(jnp.int32, (SUB, LEV), 0)
    val = jnp.where(sub >= 1, pltpu.roll(val, 1, 0), 0.0)
    for step in (1, 2, 4):
        val = val + jnp.where(sub >= step, pltpu.roll(val, step, 0), 0.0)
    return val


def sums_after(val):
    sub = lax.broadcasted_iota(jnp.int32, (SUB, LEV), 0)
    val = jnp.where(sub < SUB - 1, pltpu.roll(val, SUB - 1, 0), 0.0)
    for step in (1, 2, 4):
        val = val + jnp.where(sub < SUB - step, pltpu.roll(val, SUB - step, 0), 0.0)
    return val


def kernel(
    e_hbm, g_hbm, norm_hbm, lon_hbm, lat_hbm, diag_hbm, below_hbm, out_v,
    e_v, g_v, norm_ref, lon_ref, lat_ref, diag_ref, below_ref, y_v,
    tmp, rk_t, phi_t, w1_t, n_t, phin_t, w1n_t,
    w1n_e, phin_e, w1_e, phi_e,
    lat_pad, lat_rk, lat_rows, lat_t, w1l_e, phil_e, cw1_e, cphi_e,
    vinv,
    cs_a, cr_a, ss_a, sr_a, ts_a, tr_a, rows_a, inv_a,
    cs_b, cr_b, ss_b, sr_b, ts_b, tr_b, rows_b, tb_b, el_b,
    load_sem,
    ca_send, ca_recv, sa_send, sa_recv, ta_send, ta_recv,
    cb_send, cb_recv, sb_send, sb_recv, tb_send, tb_recv,
):
    band = lax.axis_index("lat")
    me = lax.axis_index("lon")
    is_solver = jnp.logical_and(me >= FIRST, me < FIRST + SOLVERS)
    place = (me + SOLVERS - FIRST) % SOLVERS
    seat = (me + BLOCKS - FIRST) % BLOCKS

    barrier = pltpu.get_barrier_semaphore()

    def greet_lon(step, _):
        away = BLOCKS // 2 + (step + 1) // 2 * (1 - step % 2 * 2)
        pl.semaphore_signal(barrier, inc=1, device_id=(band, (me + away) % BLOCKS), device_id_type=MESH)
        return 0

    def greet_lat(step, _):
        pl.semaphore_signal(barrier, inc=1, device_id=((band + step) % BANDS, me), device_id_type=MESH)
        return 0

    @pl.when(is_solver)
    def _():
        lax.fori_loop(0, BLOCKS - 1, greet_lon, 0)

    pairs = (
        (lon_hbm, lon_ref), (norm_hbm, norm_ref), (lat_hbm, lat_ref), (g_hbm, g_v), (e_hbm, e_v),
        (diag_hbm, diag_ref), (below_hbm, below_ref),
    )
    loads = [pltpu.make_async_copy(*pair, load_sem.at[k]) for k, pair in enumerate(pairs)]
    for copy in loads:
        copy.start()

    lax.fori_loop(1, BANDS, greet_lat, 0)

    tmp[...] = jnp.full((LEV, LEV), 2048.0, F32)
    loads[0].wait()
    loads[1].wait()
    tmp[0:ROWS, 0:COLS] = lon_ref[...]
    rk_t[...] = 1.0 / tmp[...].T[0:COLS]
    tmp[0:ROWS, 0:COLS] = norm_ref[...]
    n_t[...] = tmp[...].T[0:COLS]
    flow_p = jnp.zeros((1, LEV), F32)
    flow_s = jnp.zeros((1, LEV), F32)
    val_p = rk_t[0:1]
    val_s = rk_t[COLS - 1 : COLS]
    phi_t[0:1] = jnp.zeros((1, LEV), F32)
    phi_t[1:2] = val_p
    w1_t[COLS - 1 : COLS] = val_s
    for i in range(1, COLS):
        flow_p = flow_p + val_p
        val_p = val_p + (1.0 + flow_p) * rk_t[i : i + 1]
        if i < COLS - 1:
            phi_t[i + 1 : i + 2] = val_p
        k = COLS - i
        flow_s = flow_s + val_s
        val_s = val_s + (1.0 + flow_s) * rk_t[k - 1 : k]
        w1_t[k - 1 : k] = val_s
    edge = 1.0 / val_p
    scale = 1.0 / val_s
    lane = lax.broadcasted_iota(jnp.int32, (SUB, LEV), 1)
    own = pltpu.roll(wide(1.0 + flow_s * scale), 16, 1)
    after = pltpu.roll(wide(flow_p * edge), 32, 1)
    cs_a[...] = jnp.where(lane < 16, wide(edge), jnp.where(lane < 32, own, after))
    w1_t[...] = w1_t[...] * scale
    w1n_t[...] = w1_t[...] * n_t[...]
    phin_t[...] = phi_t[...] * n_t[...]

    @pl.when(is_solver)
    def _():
        pl.semaphore_wait(barrier, SOLVERS + BANDS - 2)

    @pl.when(jnp.logical_not(is_solver))
    def _():
        pl.semaphore_wait(barrier, SOLVERS + BANDS - 1)

    def coeff_copy_a(solver):
        return pltpu.make_async_remote_copy(
            src_ref=cs_a.at[pl.ds(0, 1)],
            dst_ref=cr_a.at[pl.ds(me, 1)],
            send_sem=ca_send.at[solver],
            recv_sem=ca_recv,
            device_id=(band, solver + FIRST),
            device_id_type=MESH,
        )

    def rhs_copy_a(solver):
        return pltpu.make_async_remote_copy(
            src_ref=ss_a.at[rows_at(solver * PACK, PACK)],
            dst_ref=sr_a.at[rows_at(me * PACK, PACK)],
            send_sem=sa_send.at[solver],
            recv_sem=sa_recv,
            device_id=(band, solver + FIRST),
            device_id_type=MESH,
        )

    def back_copy_a(target):
        return pltpu.make_async_remote_copy(
            src_ref=ts_a.at[rows_at(target * PACK, PACK)],
            dst_ref=tr_a.at[rows_at(place * PACK, PACK)],
            send_sem=ta_send.at[target],
            recv_sem=ta_recv.at[place],
            device_id=(band, target),
            device_id_type=MESH,
        )

    def copy_b(kind, target):
        size = SUB if kind == 0 else 2 * HALF
        source = (cs_b, ss_b, ts_b)[kind]
        dest = (cr_b, sr_b, tr_b)[kind]
        return pltpu.make_async_remote_copy(
            src_ref=source if kind == 0 else source.at[rows_at(target * size, size)],
            dst_ref=dest.at[rows_at(band * size, size)],
            send_sem=(cb_send, sb_send, tb_send)[kind].at[target],
            recv_sem=(cb_recv, sb_recv, tb_recv)[kind].at[band],
            device_id=(target, me),
            device_id_type=MESH,
        )

    def landed_b(kind, source):
        size = SUB if kind == 0 else 2 * HALF
        dest = (cr_b, sr_b, tr_b)[kind]
        slot = dest.at[rows_at(source * size, size)]
        return pltpu.make_async_copy(slot, slot, (cb_recv, sb_recv, tb_recv)[kind].at[source])

    def send_coeff_a(step, _):
        solver = (me + step) % SOLVERS

        @pl.when(solver != seat)
        def _():
            coeff_copy_a(solver).start()

        return 0

    lax.fori_loop(0, SOLVERS, send_coeff_a, 0)

    @pl.when(is_solver)
    def _():
        cr_a[pl.ds(me, 1)] = cs_a[0:1]

    for t in range(RUN):
        for source, target in ((w1n_t, w1n_e), (phin_t, phin_e)):
            part = source[pl.ds(t, SUB, stride=RUN), :]
            for j in range(ROWS):
                at = j * COLS + t * SUB
                target[at : at + SUB] = jnp.broadcast_to(part[:, j : j + 1], (SUB, LEV))

    loads[3].wait()
    loads[4].wait()

    def contribute(step, _):
        solver = (me + step) % SOLVERS
        for g in range(GROUP):
            row = solver * GROUP + g
            sums = [jnp.zeros((SUB, LEV), F32) for _ in range(2 * MEMB)]
            for t in range(RUN):
                grad = g_v[pl.ds(row * COLS + t, SUB, stride=RUN), :]
                first = w1n_e[rows_at(row * COLS + t * SUB)] * grad
                second = phin_e[rows_at(row * COLS + t * SUB)] * grad
                for m in range(MEMB):
                    value = e_v[pl.ds(row * COLS * MEMB + t * MEMB + m, SUB, stride=RUN * MEMB), :]
                    sums[m] = sums[m] + first * value
                    sums[MEMB + m] = sums[MEMB + m] + second * value
            ss_a[rows_at(row * SUB)] = sublane_sums(sums)

        @pl.when(solver != seat)
        def _():
            rhs_copy_a(solver).start()

        return 0

    lax.fori_loop(0, SOLVERS, contribute, 0, unroll=2)

    @pl.when(is_solver)
    def _():
        sr_a[rows_at(me * PACK, PACK)] = ss_a[rows_at(place * PACK, PACK)]

    lat_pad[...] = jnp.full((16, LEV), 512.0, F32)
    loads[2].wait()
    lat_pad[0:ROWS, 0:COLS] = lat_ref[...]
    lat_rk[...] = 1.0 / lat_pad[...]
    at = band * ROWS + lax.broadcasted_iota(jnp.int32, (16, LEV), 0)
    at = jnp.minimum(at, NLAT - 1 - at).astype(F32)
    angle = (at + 0.5) * (math.pi / NLAT)
    square = angle * angle
    series = jnp.full((16, LEV), 1.0 / math.factorial(13), F32)
    for power in (11, 9, 7, 5, 3, 1):
        series = 1.0 / math.factorial(power) - series * square
    lat_t[0:16] = angle * series

    def cosine(j):
        return lat_t[j : j + 1]

    last = jnp.where(band == BANDS - 1, 0.0, 1.0) * lat_pad[ROWS - 1 : ROWS]
    lat_rows[...] = jnp.zeros((LEV, LEV), F32)
    flow_p = jnp.zeros((1, LEV), F32)
    flow_s = jnp.zeros((1, LEV), F32)
    val_p = lat_rk[0:1]
    val_s = jnp.ones((1, LEV), F32)
    lat_rows[17:18] = val_p
    lat_rows[ROWS - 1 : ROWS] = val_s
    for j in range(1, ROWS):
        flow_p = flow_p + cosine(j) * val_p
        if j < ROWS - 1:
            val_p = val_p + (1.0 + flow_p) * lat_rk[j : j + 1]
            lat_rows[17 + j : 18 + j] = val_p
        k = ROWS - j
        flow_s = flow_s + cosine(k) * val_s
        val_s = val_s + (last + flow_s) * lat_rk[k - 1 : k]
        lat_rows[k - 1 : k] = val_s
    edge = last / (last * val_p + 1.0 + flow_p)
    scale = 1.0 / val_s
    cs_b[...] = jnp.zeros((SUB, LEV), F32)
    cs_b[0:1] = edge
    cs_b[1:2] = cosine(0) + flow_s * scale
    cs_b[2:3] = flow_p * edge
    lat_rows[0:16] = lat_rows[0:16] * scale
    lat_rows[32:48] = lat_rows[0:16] * lat_t[0:16]
    lat_rows[48:64] = lat_rows[16:32] * lat_t[0:16]

    def send_coeff_b(step, _):
        copy_b(0, (band + step) % BANDS).start()
        return 0

    lax.fori_loop(1, BANDS, send_coeff_b, 0)
    cr_b[rows_at(band * SUB)] = cs_b[...]

    loads[5].wait()
    loads[6].wait()
    tmp[0:SUB] = jnp.zeros((SUB, LEV), F32)
    tmp[0:1, 0 : LEV - 1] = below_ref[...]
    dinv = 1.0 / wide(diag_ref[...])
    lane = lax.broadcasted_iota(jnp.int32, (SUB, LEV), 1)
    ratio = jnp.where(lane == 0, 0.0, -pltpu.roll(wide(tmp[0:1]), 1, 1) * dinv)
    row_ids = lax.broadcasted_iota(jnp.int32, (LEV, LEV), 0)
    col_ids = lax.broadcasted_iota(jnp.int32, (LEV, LEV), 1)
    half = jnp.where(row_ids == col_ids, wide(dinv[0:1], LEV), 0.0)
    step = 1
    while step < LEV:
        half = half + wide(ratio[0:1], LEV) * pltpu.roll(half, step, 1)
        ratio = ratio * pltpu.roll(ratio, step, 1)
        step *= 2
    vinv[...] = lax.dot_general(
        half, half, (((1,), (1,)), ((), ())), precision=HIGHEST, preferred_element_type=F32
    )

    for t in range(RUN):
        for source, target in ((w1_t, w1_e), (phi_t, phi_e)):
            part = source[pl.ds(t, SUB, stride=RUN), :]
            for j in range(ROWS):
                at = j * COLS + t * SUB
                target[at : at + SUB] = jnp.broadcast_to(part[:, j : j + 1], (SUB, LEV))

    def interior(row, _):
        firsts, seconds = [], []
        for t in range(RUN):
            grad = g_v[pl.ds(row * COLS + t, SUB, stride=RUN), :]
            firsts.append(w1n_e[rows_at(row * COLS + t * SUB)] * grad)
            seconds.append(phin_e[rows_at(row * COLS + t * SUB)] * grad)
        for m in range(MEMB):
            values = [
                e_v[pl.ds(row * COLS * MEMB + t * MEMB + m, SUB, stride=RUN * MEMB), :] for t in range(RUN)
            ]
            ahead = [seconds[0] * values[0]]
            for t in range(1, RUN):
                ahead.append(ahead[-1] + seconds[t] * values[t])
            behind = [None] * RUN
            total = jnp.zeros((SUB, LEV), F32)
            for t in reversed(range(RUN)):
                behind[t] = total
                total = total + firsts[t] * values[t]
            before = sums_before(ahead[-1])
            after = sums_after(total)
            for t in range(RUN):
                w1 = w1_e[rows_at(row * COLS + t * SUB)]
                phi = phi_e[rows_at(row * COLS + t * SUB)]
                y_v[rows_at(((m * RUN + t) * ROWS + row) * SUB)] = w1 * (before + ahead[t]) + phi * (
                    after + behind[t]
                )
        return 0

    lax.fori_loop(0, ROWS, interior, 0)

    size = UNITS * SUB

    def vertical(part, _):
        at = rows_at(part * size, size)
        y_v[at] = jnp.dot(y_v[at], vinv[...], precision=HIGHEST, preferred_element_type=F32)
        return 0

    lax.fori_loop(0, ROWS, vertical, 0)

    lat_t[...] = lat_rows[...].T
    for t in range(RUN):
        part = lat_t[pl.ds(t, SUB, stride=RUN), :]
        for number, target in enumerate((w1l_e, phil_e, cw1_e, cphi_e)):
            for j in range(ROWS):
                at = j * COLS + t * SUB
                lane_at = number * 16 + j
                target[at : at + SUB] = jnp.broadcast_to(part[:, lane_at : lane_at + 1], (SUB, LEV))

    def wait_coeff_b(step, _):
        landed_b(0, (band + step) % BANDS).wait()
        return 0

    lax.fori_loop(1, BANDS, wait_coeff_b, 0)
    flow_p = jnp.zeros((1, LEV), F32)
    flow_s = jnp.zeros((1, LEV), F32)
    val_p = jnp.ones((1, LEV), F32)
    val_s = jnp.ones((1, LEV), F32)

    def band_base(p):
        own = cr_b[p * SUB + 1 : p * SUB + 2]
        return own if p == 0 else own + cr_b[(p - 1) * SUB + 2 : (p - 1) * SUB + 3]

    def band_link(p):
        return cr_b[p * SUB : p * SUB + 1]

    rows_b[...] = jnp.zeros((LEV, LEV), F32)
    rows_b[0:1] = val_p
    rows_b[2 * BANDS - 1 : 2 * BANDS] = val_s
    for p in range(BANDS - 1):
        flow_p = flow_p + band_base(p) * val_p
        val_p = val_p + flow_p / band_link(p)
        rows_b[p + 1 : p + 2] = val_p
        k = BANDS - 1 - p
        flow_s = flow_s + band_base(k) * val_s
        val_s = val_s + flow_s / band_link(k - 1)
        rows_b[BANDS + k - 1 : BANDS + k] = val_s
    flow_s = flow_s + band_base(0) * val_s
    rows_b[BANDS : 2 * BANDS] = rows_b[BANDS : 2 * BANDS] * (1.0 / flow_s)
    for p in range(BANDS - 1):
        rows_b[2 * BANDS + p : 2 * BANDS + p + 1] = band_link(p)
    tb_b[...] = rows_b[...].T
    for tt in range(SHARE):
        part = tb_b[pl.ds((band % 2) * SHARE + tt, SUB, stride=RUN), :]
        for number in range(3 * BANDS):
            at = (number * SHARE + tt) * SUB
            el_b[at : at + SUB] = jnp.broadcast_to(part[:, number : number + 1], (SUB, LEV))

    @pl.when(is_solver)
    def _():
        slots = cr_a.at[pl.ds(0, BLOCKS - 1)]
        pltpu.make_async_copy(slots, slots, ca_recv).wait()
        link = cr_a[...]
        base = pltpu.roll(link, LEV - 16, 1) + pltpu.roll(pltpu.roll(link, LEV - 32, 1), 1, 0)
        rows_a[0:BLOCKS] = 1.0 / link
        rows_a[BLOCKS : 2 * BLOCKS] = base
        flow_p = jnp.zeros((1, LEV), F32)
        flow_s = jnp.zeros((1, LEV), F32)
        val_p = rows_a[0:1]
        val_s = rows_a[BLOCKS - 1 : BLOCKS]
        tmp[0:1] = jnp.zeros((1, LEV), F32)
        tmp[1:2] = val_p
        tmp[2 * BLOCKS - 1 : 2 * BLOCKS] = val_s
        for p in range(1, BLOCKS):
            flow_p = flow_p + rows_a[BLOCKS + p : BLOCKS + p + 1] * val_p
            val_p = val_p + (1.0 + flow_p) * rows_a[p : p + 1]
            if p < BLOCKS - 1:
                tmp[p + 1 : p + 2] = val_p
            k = BLOCKS - p
            flow_s = flow_s + rows_a[BLOCKS + k : BLOCKS + k + 1] * val_s
            val_s = val_s + (1.0 + flow_s) * rows_a[k - 1 : k]
            tmp[BLOCKS + k - 1 : BLOCKS + k] = val_s
        first = tmp[BLOCKS : 2 * BLOCKS] * (1.0 / val_s)
        both = first + tmp[0:BLOCKS] * (1.0 / val_p)
        total = jnp.sum(both * base, axis=0, keepdims=True)
        tmp[BLOCKS : 2 * BLOCKS] = first
        tmp[2 * BLOCKS : 3 * BLOCKS] = both * (1.0 / total)
        tmp[3 * BLOCKS : 4 * BLOCKS] = both
        whole = tmp[...]
        lanes = lax.broadcasted_iota(jnp.int32, (LEV, LEV), 1)
        columns = []
        for g in range(GROUP):
            column = jnp.sum(jnp.where(lanes == place * GROUP + g, whole, 0.0), axis=1, keepdims=True)
            columns.append(jnp.broadcast_to(column, (LEV, LEV)))
        tmp[...] = whole.T
        sub_ids = lax.broadcasted_iota(jnp.int32, (BLOCKS, LEV), 0)
        lane_ids = lax.broadcasted_iota(jnp.int32, (BLOCKS, LEV), 1)
        for g, column in enumerate(columns):
            line = wide(tmp[pl.ds(place * GROUP + g, 1), :])
            phi_row = wide(line[0:1], BLOCKS)
            first_row = wide(pltpu.roll(line, LEV - BLOCKS, 1)[0:1], BLOCKS)
            both_row = wide(pltpu.roll(line, LEV - 2 * BLOCKS, 1)[0:1], BLOCKS)
            at = 2 * g * BLOCKS
            inv_a[at : at + BLOCKS] = (
                jnp.where(
                    sub_ids <= lane_ids,
                    column[0:BLOCKS] * first_row,
                    column[BLOCKS : 2 * BLOCKS] * phi_row,
                )
                + column[3 * BLOCKS : 4 * BLOCKS] * both_row
            )
            edge = jnp.sum(jnp.where(lane_ids == place * GROUP + g, link, 0.0), axis=1, keepdims=True)
            inv_a[at + BLOCKS : at + 2 * BLOCKS] = jnp.broadcast_to(edge, (BLOCKS, LEV))

    @pl.when(is_solver)
    def _():
        vinv_high, vinv_low = parts_of(vinv[...])
        slots = sr_a.at[rows_at(0, (BLOCKS - 1) * PACK)]
        pltpu.make_async_copy(slots, slots, sa_recv).wait()
        for g in range(GROUP):
            inverse = inv_a[2 * g * BLOCKS : (2 * g + 1) * BLOCKS]
            link = inv_a[(2 * g + 1) * BLOCKS : (2 * g + 2) * BLOCKS]
            inv_high, inv_low = parts_of(inverse[:, 0:BLOCKS])
            rhs = []
            for m in range(MEMB):
                own = sr_a[pl.ds(g * SUB + m, BLOCKS, stride=PACK), :]
                after = sr_a[pl.ds(g * SUB + MEMB + m, BLOCKS, stride=PACK), :]
                rhs.append(own + pltpu.roll(link * after, 1, 0))
            high, low = parts_of(jnp.concatenate(rhs, axis=0))
            rhs = product(high, vinv_high) + product(high, vinv_low) + product(low, vinv_high)
            high, low = parts_of(
                jnp.concatenate([rhs[m * BLOCKS : (m + 1) * BLOCKS] for m in range(MEMB)], axis=1)
            )
            solved = product(inv_high, high) + product(inv_high, low) + product(inv_low, high)
            for m in range(MEMB):
                found = solved[:, m * LEV : (m + 1) * LEV]
                ts_a[pl.ds(g * SUB + m, BLOCKS, stride=PACK), :] = found
                ts_a[pl.ds(g * SUB + MEMB + m, BLOCKS, stride=PACK), :] = link * pltpu.roll(found, BLOCKS - 1, 0)

        def send_back(target, _):
            @pl.when(target != me)
            def _():
                back_copy_a(target).start()

            return 0

        lax.fori_loop(0, BLOCKS, send_back, 0)
        tr_a[rows_at(place * PACK, PACK)] = ts_a[rows_at(me * PACK, PACK)]

    def wait_back_a(solver, _):
        @pl.when(solver != seat)
        def _():
            slot = tr_a.at[rows_at(solver * PACK, PACK)]
            pltpu.make_async_copy(slot, slot, ta_recv.at[solver]).wait()

        return 0

    lax.fori_loop(0, SOLVERS, wait_back_a, 0)

    def finish_lon(step, _):
        share = lat_partner(band, step)
        m = share // 2
        for tt in range(SHARE):
            t = (share % 2) * SHARE + tt
            own = jnp.zeros((SUB, LEV), F32)
            after = jnp.zeros((SUB, LEV), F32)
            for j in range(ROWS):
                at = rows_at(((share * SHARE + tt) * ROWS + j) * SUB)
                coeff = rows_at(j * COLS + t * SUB)
                sep_own = wide(tr_a[pl.ds(j * SUB + m, 1), :])
                sep_next = wide(tr_a[pl.ds(j * SUB + MEMB + m, 1), :])
                value = y_v[at] + w1_e[coeff] * sep_own + phi_e[coeff] * sep_next
                y_v[at] = value
                own = own + w1l_e[coeff] * value
                after = after + phil_e[coeff] * value
            ss_b[rows_at(share * 2 * HALF + tt * SUB)] = own
            ss_b[rows_at(share * 2 * HALF + HALF + tt * SUB)] = after

        @pl.when(share != band)
        def _():
            copy_b(1, share).start()

        return 0

    lax.fori_loop(0, BANDS, finish_lon, 0)
    sr_b[rows_at(band * 2 * HALF, 2 * HALF)] = ss_b[rows_at(band * 2 * HALF, 2 * HALF)]

    def interior_lat(unit, _):
        t = unit % RUN
        total = jnp.zeros((SUB, LEV), F32)
        aheads = []
        for j in range(ROWS):
            at = rows_at((unit * ROWS + j) * SUB)
            total = total + phil_e[rows_at(j * COLS + t * SUB)] * y_v[at]
            aheads.append(total)
        total = jnp.zeros((SUB, LEV), F32)
        for j in reversed(range(ROWS)):
            at = rows_at((unit * ROWS + j) * SUB)
            coeff = rows_at(j * COLS + t * SUB)
            value = y_v[at]
            y_v[at] = cw1_e[coeff] * aheads[j] + cphi_e[coeff] * total
            total = total + w1l_e[coeff] * value
        return 0

    lax.fori_loop(0, UNITS, interior_lat, 0)

    def wait_rhs_b(step, _):
        landed_b(1, (band + step) % BANDS).wait()
        return 0

    lax.fori_loop(1, BANDS, wait_rhs_b, 0)

    for tt in range(SHARE):

        def spread(number):
            at = (number * SHARE + tt) * SUB
            return el_b[at : at + SUB]

        rhs = []
        total = jnp.zeros((SUB, LEV), F32)
        aheads = []
        for p in range(BANDS):
            at = p * 2 * HALF + tt * SUB
            value = sr_b[at : at + SUB]
            if p > 0:
                before = at - HALF
                value = value + spread(2 * BANDS + p - 1) * sr_b[before : before + SUB]
            rhs.append(value)
            total = total + spread(p) * value
            aheads.append(total)
        total = jnp.zeros((SUB, LEV), F32)
        found = None
        for p in reversed(range(BANDS)):
            at = p * 2 * HALF + tt * SUB
            if p == BANDS - 1:
                ts_b[at + HALF : at + HALF + SUB] = jnp.zeros((SUB, LEV), F32)
            else:
                ts_b[at + HALF : at + HALF + SUB] = spread(2 * BANDS + p) * found
            found = spread(BANDS + p) * aheads[p] + spread(p) * total
            ts_b[at : at + SUB] = found
            total = total + spread(BANDS + p) * rhs[p]

    def send_back_b(step, _):
        target = (2 * step + 1 - step // (BANDS // 2)) % BANDS

        @pl.when(target != band)
        def _():
            copy_b(2, target).start()

        return 0

    lax.fori_loop(0, BANDS, send_back_b, 0)
    tr_b[rows_at(band * 2 * HALF, 2 * HALF)] = ts_b[rows_at(band * 2 * HALF, 2 * HALF)]

    def sent_a(solver, _):
        @pl.when(solver != seat)
        def _():
            coeff_copy_a(solver).wait_send()
            rhs_copy_a(solver).wait_send()

        return 0

    lax.fori_loop(0, SOLVERS, sent_a, 0)

    @pl.when(is_solver)
    def _():
        def sent_back(step, _):
            back_copy_a((me + step) % BLOCKS).wait_send()
            return 0

        lax.fori_loop(1, BLOCKS, sent_back, 0)

    def sent_b(step, _):
        for kind in range(3):
            copy_b(kind, (band + step) % BANDS).wait_send()
        return 0

    lax.fori_loop(1, BANDS, sent_b, 0)

    def finish(step, _):
        share = lat_partner(band, BANDS - 1 - step)

        @pl.when(share != band)
        def _():
            landed_b(2, share).wait()

        m = share // 2
        for tt in range(SHARE):
            t = (share % 2) * SHARE + tt
            sep_own = tr_b[rows_at(share * 2 * HALF + tt * SUB)]
            sep_next = tr_b[rows_at(share * 2 * HALF + HALF + tt * SUB)]
            for j in range(ROWS):
                at = rows_at(((share * SHARE + tt) * ROWS + j) * SUB)
                coeff = rows_at(j * COLS + t * SUB)
                out_v[pl.ds(j * COLS * MEMB + t * MEMB + m, SUB, stride=RUN * MEMB), :] = (
                    y_v[at] + cw1_e[coeff] * sep_own + cphi_e[coeff] * sep_next
                )
        return 0

    lax.fori_loop(0, BANDS, finish, 0)


def shards(
    ensemble, grad_increment, normalization, lon_diffusion, lat_diffusion, vert_diag, vert_sub
):
    block = ROWS * COLS * MEMB
    anywhere = pl.BlockSpec(memory_space=pl.ANY)

    def buf(rows):
        return pltpu.VMEM((rows, LEV), F32)

    coeffs = ROWS * COLS
    dma = pltpu.SemaphoreType.DMA
    scratch = [
        buf(block), buf(coeffs), *[pltpu.VMEM((ROWS, COLS), F32)] * 3, buf(1), pltpu.VMEM((1, LEV - 1), F32),
        buf(block),
        buf(LEV), *[buf(COLS)] * 6,
        *[buf(coeffs)] * 4,
        buf(16), buf(16), buf(LEV), buf(LEV), *[buf(coeffs)] * 4,
        buf(LEV),
        buf(SUB), buf(BLOCKS), buf(ROWS * SUB), buf(BLOCKS * PACK), buf(BLOCKS * PACK), buf(ROWS * SUB),
        buf(2 * BLOCKS), buf(2 * GROUP * BLOCKS),
        buf(SUB), buf(BANDS * SUB), *[buf(BANDS * 2 * HALF)] * 4,
        buf(LEV), buf(LEV), buf(3 * BANDS * HALF),
        dma((7,)),
        dma((SOLVERS,)), dma, dma((SOLVERS,)), dma, dma((BLOCKS,)), dma((SOLVERS,)),
        *[dma((BANDS,))] * 6,
    ]
    out = pl.pallas_call(
        kernel,
        out_shape=pltpu.VMEM((block, LEV), F32),
        in_specs=[anywhere] * 7,
        out_specs=pl.BlockSpec(memory_space=pltpu.VMEM),
        scratch_shapes=scratch,
        compiler_params=pltpu.CompilerParams(
            collective_id=0, has_side_effects=True, vmem_limit_bytes=60 * 1024 * 1024
        ),
    )(
        ensemble.reshape(block, LEV),
        grad_increment.reshape(coeffs, LEV),
        normalization,
        lon_diffusion,
        lat_diffusion,
        vert_diag.reshape(1, LEV),
        vert_sub.reshape(1, LEV - 1),
    )
    return out.reshape(ROWS, COLS, MEMB, LEV)


def solution(mesh):
    in_specs = (
        P("lat", "lon", None, None),
        P("lat", "lon", None),
        P("lat", "lon"),
        P("lat", "lon"),
        P("lat", "lon"),
        P(),
        P(),
    )
    out_specs = P("lat", "lon", None, None)
    return jax.shard_map(shards, mesh=mesh, in_specs=in_specs, out_specs=out_specs, check_vma=False)
```
